128 devices in a mesh: node: 8 (over z, core), local: 16 (over x, y).
Axes of the slice: x: 4, y: 4, z: 4, core: 2. Of those that a mesh axis runs over, the one named last changes fastest.
Arguments:
- tokens: bfloat16 [256, 7168], P(('node', 'local')), may hold values from -6 to 6
- gates: bfloat16 [256, 8], P(('node', 'local')), may hold values from 0.049804688 to 0.5
- node_set: int32 [256, 4], P(('node', 'local')), may hold values from 0 to 7, all different within a row; in each aligned block of 2 rows (0 to 1, 2 to 3, ...) at most 2 rows name the same one
- w_gate: bfloat16 [7168, 32768], P(None, ('node', 'local')), may hold values from -0.0625 to 0.0625
- w_up: bfloat16 [7168, 32768], P(None, ('node', 'local')), may hold values from -0.0625 to 0.0625
- w_down: bfloat16 [32768, 7168], P(('node', 'local')), may hold values from -0.125 to 0.125
Outputs:
- mixed: bfloat16 [256, 7168], P(('node', 'local'))
The draws below stay inside these ranges and needn't reach their ends.
Inputs may be any that keep to these rules, and one draw needn't show every extreme that they name: `node_set`: each row names 4 different nodes; among the rows of one device at most 2 name the same node, and in every draw some node is named by exactly 2 rows of some device.
All inputs are finite; a program needn't handle non-finite values.
Results may differ from the reference program's by a relative error of at most 0.005.
Values may be sent and summed in bfloat16 or wider, within the bound.
A program may use at most 64 MiB of HBM per device.

```python
import math
import jax
import jax.numpy as jnp
import numpy as np
from jax import lax

D = 7168
FF = 2048
TOK_DEV = 2
NLIM = 4
E_NODE = 2
EXPERTS = 16
TOP = 8
CAP = 2
TOKENS = 256
N_NODE = 8
N_LOCAL = 16


def level_of(rng, shape, cuts, low, largest):
    gain, own = 1.0, jax.random.fold_in(rng, 6)
    for axis_at, parts in cuts:
        heights = jnp.exp(jax.random.uniform(jax.random.fold_in(own, axis_at), (parts,), jnp.float32, low / len(cuts), largest / len(cuts)))
        gain = gain * jnp.repeat(heights, shape[axis_at] // parts).reshape([-1 if axis == axis_at else 1 for axis in range(len(shape))])
    return gain


def shared_out(stream_key, own, number, rows, amount, top, most, slope):
    order = jax.random.permutation(stream_key, amount)
    packed, usual = portions_of(amount, rows * top, most, slope, True), portions_of(amount, rows * top, most, slope, False)
    places = jnp.arange(amount)

    def named(tallies, offset_by):
        used = int((tallies > 0).sum())
        fixed = max(1, used // 4)
        moved = fixed + (places - fixed + offset_by * (used - fixed)) % max(1, amount - fixed)
        return jnp.zeros((amount,), jnp.int32).at[order[jnp.where(places < fixed, places, moved)]].set(jnp.asarray(tallies, jnp.int32))

    tallies = jnp.where(number % 4 == 0, named(packed, number // 4), named(usual, number - number // 4 - 1))
    mixed = jax.random.permutation(jax.random.fold_in(own, 3), amount)
    source_of, receiver = mixed[0:amount // 2 * 2:2], mixed[1:amount // 2 * 2:2]
    slack = jnp.minimum(tallies[source_of] - 1, most - tallies[receiver]) // 2
    slack = jnp.where((source_of == order[0]) | (receiver == order[0]) | (tallies[receiver] == 0), 0, jnp.maximum(slack, 0))
    moved = jax.random.randint(jax.random.fold_in(own, 4), (amount // 2,), 0, 1 << 20) % (slack + 1)
    tallies = tallies.at[source_of].add(-moved).at[receiver].add(moved)
    items = jnp.searchsorted(jnp.cumsum(tallies), jnp.arange(rows * top), side="right").astype(jnp.int32)
    table = items.reshape(top, rows).T
    table = table[jax.random.permutation(jax.random.fold_in(own, 1), rows)]
    offset_by = jax.random.randint(jax.random.fold_in(own, 2), (rows, 1), 0, top)
    return jnp.take_along_axis(table, (jnp.arange(top)[None, :] + offset_by) % top, axis=1)


def portions_of(number_of, total, bound, lean, full):
    weights = [(1 << 20) // math.isqrt(standing ** lean) + 1 for standing in range(1, number_of + 1)]
    largest = bound if full else min(bound, max(-(-total // number_of), total * weights[0] // sum(weights)))
    least = 1 if total - largest >= number_of - 1 else 0
    counts, spare = [largest] + [least] * (number_of - 1), total - largest - least * (number_of - 1)
    while spare > 0:
        candidates = [i for i in range(1, number_of) if counts[i] < largest] or [i for i in range(1, number_of) if counts[i] < bound]
        pool, budget = sum([weights[i] for i in candidates]), spare
        for i in candidates:
            addition = min(bound - counts[i], max(1, budget * weights[i] // pool), spare)
            counts[i] = counts[i] + addition
            spare = spare - addition
    return np.array(counts)


def gaussian(key, shape, width, reach, shards=(), kind=jnp.bfloat16):
    loudness = level_of(key, shape, shards, -0.22, 0.18) if shards else 1.0
    result = jax.random.normal(key, shape, jnp.float32) * width * loudness
    return jnp.minimum(jnp.maximum(result, -reach), reach).astype(kind)


def setup_inputs(seed: int = 0) -> dict:
    splits = jax.random.split(jax.random.key(seed), 7)
    tokens = gaussian(splits[0], (TOKENS, D), 1.0, 6.0, ((0, 128),))
    gates = jnp.clip(jnp.exp(math.log(0.5) - 2.306499 * jax.random.uniform(splits[1], (TOKENS, TOP), jnp.float32) ** level_of(splits[1], (TOKENS, TOP), ((0, 128),), -0.2, 0.2)), 0.049804688, 0.5).astype(jnp.bfloat16)
    node_set_keys = jax.random.split(jax.random.fold_in(splits[2], 1), TOKENS // TOK_DEV)
    node_set_turns = jax.random.permutation(jax.random.fold_in(splits[2], 3), TOKENS // TOK_DEV)
    node_set = jax.vmap(lambda own, number: shared_out(jax.random.fold_in(splits[2], 2), own, number, TOK_DEV, N_NODE, NLIM, CAP, 2))(node_set_keys, node_set_turns).reshape((TOKENS, NLIM))
    w_gate = gaussian(splits[3], (D, EXPERTS * FF), D ** -0.5, 0.0625, ((1, 128),))
    w_up = gaussian(splits[4], (D, EXPERTS * FF), D ** -0.5, 0.0625, ((1, 128),))
    w_down = gaussian(splits[5], (EXPERTS * FF, D), FF ** -0.5, 0.125, ((0, 128),))
    return {"tokens": tokens, "gates": gates, "node_set": node_set, "w_gate": w_gate, "w_up": w_up, "w_down": w_down}


def expert_output(rows_in, gate_column, part_gate, part_up, part_down):
    gate_pre = jnp.dot(rows_in, part_gate, preferred_element_type=jnp.float32)
    up_pre = jnp.dot(rows_in, part_up, preferred_element_type=jnp.float32)
    hidden_act = (gate_pre * jax.nn.sigmoid(gate_pre) * up_pre).astype(jnp.bfloat16)
    expert_out = jnp.dot(hidden_act, part_down, preferred_element_type=jnp.float32)
    return gate_column[:, None] * expert_out


def reference(tokens, gates, node_set, w_gate, w_up, w_down):
    expert_count = N_NODE * E_NODE
    row_limit = N_NODE * N_LOCAL * CAP
    gate_table = gates.astype(jnp.float32).reshape(TOKENS, NLIM, E_NODE)

    def one_expert(carry, expert):
        node_index = expert // E_NODE
        place_index = expert % E_NODE
        node_match = (node_set == node_index)
        node_hit = node_match.astype(jnp.float32)
        pick_column = (jnp.arange(E_NODE, dtype=jnp.int32) == place_index).astype(jnp.float32)
        weight = jnp.einsum("tj,tje,e->t", node_hit, gate_table, pick_column)
        chosen = jnp.sum(node_match.astype(jnp.int32), axis=1)
        row_order = jnp.argsort(1 - chosen, stable=True)[:row_limit].astype(jnp.int32)
        rows_in = tokens[row_order]
        gate_column = weight[row_order]
        start = (expert * FF).astype(jnp.int32)
        part_gate = lax.dynamic_slice_in_dim(w_gate, start, FF, 1)
        part_up = lax.dynamic_slice_in_dim(w_up, start, FF, 1)
        part_down = lax.dynamic_slice_in_dim(w_down, start, FF, 0)
        contribution = expert_output(rows_in, gate_column, part_gate, part_up, part_down)
        carry = carry.at[row_order].add(contribution)
        return carry, None

    initial = jnp.zeros((TOKENS, D), jnp.float32)
    mixed_sum, unused = lax.scan(one_expert, initial, jnp.arange(expert_count, dtype=jnp.int32))
    return mixed_sum.astype(jnp.bfloat16)
```

```python
import functools

import jax
import jax.numpy as jnp
from jax import lax
from jax.experimental import pallas as pl
from jax.experimental.pallas import tpu as pltpu
from jax.sharding import PartitionSpec as P

MESH = pl.DeviceIdType.MESH
SIDE = 4
ROWS = 256
TOK = 2
LINE_ROWS = 16
PLANE_ROWS = 64
LANES = 128
AHEAD = (2, 1, 3, 0)
ORDERS = ("xyz", "yzx", "zxy")
UNITS = ((0, 10), (1, 9), (2, 9))
F32, BF16 = jnp.float32, jnp.bfloat16


def widths():
    offsets, start = [], 0
    for _, blocks in UNITS:
        offsets.append(start)
        start += 2 * blocks * LANES
    return offsets, [blocks * LANES for _, blocks in UNITS]


def row_of(order, at, by_plane):
    low = at & 3
    place = dict(x=(at >> 2) & 3, y=(at >> 4) & 3, z=(at >> 6) & 3)
    first, second, third = (place[axis] for axis in ORDERS[order])
    slow, fast = (third, second) if by_plane else (second, third)
    return (((slow * SIDE + fast) * SIDE + first) << 2) + low


def kernel(tok, gates, node_set, wg, wu, wd, out, **r):
    offsets, width = widths()
    n = len(UNITS)

    node, local = lax.axis_index("node"), lax.axis_index("local")
    here = dict(x=local // SIDE, y=local % SIDE, z=node // 2)
    core = node % 2

    def device(axis, step, flip):
        at = dict(here)
        at[axis] = lax.rem(at[axis] + step, SIDE)
        other = lax.rem(core + flip, 2)
        return (at["z"] * 2 + other, at["x"] * SIDE + at["y"])

    loads = [
        pltpu.make_async_copy(wg, r["wg_v"], r["load_sem"].at[0]),
        pltpu.make_async_copy(wu, r["wu_v"], r["load_sem"].at[1]),
        pltpu.make_async_copy(wd, r["wd_v"], r["load_sem"].at[2]),
    ]
    small = [
        pltpu.make_async_copy(gates, r["gates_v"], r["small_sem"].at[0]),
        pltpu.make_async_copy(node_set, r["set_v"], r["small_sem"].at[1]),
    ]
    own = []
    for u in range(n):
        for h in range(2):
            own.append(
                pltpu.make_async_copy(
                    tok.at[:, pl.ds(offsets[u] + h * width[u], width[u])],
                    r["src"][u].at[h, :, pl.ds(0, width[u])],
                    r["tok_sem"].at[u, h],
                )
            )
    for copy in small + own:
        copy.start()

    barrier = pltpu.get_barrier_semaphore()
    partners = [(axis, step, flip) for axis in "xyz" for step in range(1, SIDE) for flip in range(2)]
    partners.append(("x", 0, 1))
    for partner in partners:
        pl.semaphore_signal(barrier, inc=1, device_id=device(*partner), device_id_type=MESH)
    for copy in loads:
        copy.start()

    for copy in small:
        copy.wait()
    lane = lax.broadcasted_iota(jnp.int32, (TOK, LANES), 1)
    table = jnp.zeros((TOK, LANES), F32)
    gate_v, set_v = r["gates_v"][...].astype(F32), r["set_v"][...]
    for j in range(set_v.shape[1]):
        pair = jnp.where(lane % 2 == 0, gate_v[:, 2 * j : 2 * j + 1], gate_v[:, 2 * j + 1 : 2 * j + 2])
        table = table + jnp.where(set_v[:, j : j + 1] == lane // 2, pair, 0.0)
    for h in range(2):
        r["src"][0][h, :, width[0] :] = table.astype(BF16)
    for copy in own:
        copy.wait()
    pl.semaphore_wait(barrier, len(partners))


    def send(src, dst, send_sem, recv_sem, to):
        copy = pltpu.make_async_remote_copy(
            src_ref=src, dst_ref=dst, send_sem=send_sem, recv_sem=recv_sem, device_id=to, device_id_type=MESH
        )
        copy.start()

    def axes(u):
        return ORDERS[UNITS[u][0]]

    def line_slot(u):
        return here[axes(u)[0]] * 2 + core

    for u in range(n):
        for step in (1, 3, 2, 0):
            for flip in range(2):
                if step or flip:
                    send(
                        r["src"][u].at[lax.rem(core + flip, 2)],
                        r["line"][u].at[line_slot(u)],
                        r["p1_send"].at[u],
                        r["p1_recv"].at[u],
                        device(axes(u)[0], step, flip),
                    )
        r["line"][u][pl.ds(line_slot(u), 1)] = r["src"][u][pl.ds(core, 1)]

    def wait_all(ref, sem):
        pltpu.make_async_copy(ref, ref, sem).wait()

    down_at = lax.broadcasted_iota(jnp.int32, (ROWS, ROWS), 0)
    across = lax.broadcasted_iota(jnp.int32, (ROWS, ROWS), 1)
    for o in (1, 2):
        r["perm"][o - 1] = (row_of(o, down_at, True) == across).astype(F32).astype(BF16)
    for o in range(3):
        r["back"][o] = (row_of(o, across, False) == down_at).astype(F32).astype(BF16)
    def plane_row(u):
        return here[axes(u)[2]] * PLANE_ROWS

    def line_block(u, back):
        second = lax.rem(here[axes(u)[1]] + SIDE - back, SIDE)
        return r["rows"][u].at[0, pl.ds(pl.multiple_of(plane_row(u) + second * LINE_ROWS, LINE_ROWS), LINE_ROWS)]

    def plane_block(u, half, back):
        third = lax.rem(here[axes(u)[2]] + SIDE - back, SIDE)
        return r["rows"][u].at[half, pl.ds(pl.multiple_of(third * PLANE_ROWS, PLANE_ROWS), PLANE_ROWS)]

    def gather3(u, back):
        for step in (2, 1, 3):
            view = line_block(u, back)
            send(view, view, r["p3_send"].at[u], r["p3_recv"].at[u, step - 1], device(axes(u)[2], step, 0))

    for u in range(n):
        wait_all(r["line"][u].at[pl.ds(0, 7)], r["p1_recv"].at[u])
        block = jnp.concatenate([r["line"][u][i].astype(F32) for i in range(8)], axis=0)
        view = line_block(u, 0)
        view[...] = block.astype(BF16)
        for step in (2, 1, 3):
            send(view, view, r["p2_send"].at[u], r["p2_recv"].at[u, step - 1], device(axes(u)[1], step, 0))
    for u in range(n):
        gather3(u, 0)
    for step in (1, 3, 2):
        for u in range(n):
            wait_all(line_block(u, step), r["p2_recv"].at[u, step - 1])
            gather3(u, step)
    for step in (0, 1, 3, 2):
        for u in range(n):
            if step:
                wait_all(plane_block(u, 0, step), r["p3_recv"].at[u, step - 1])
            send(
                plane_block(u, 0, step),
                plane_block(u, 1, step),
                r["s_send"].at[u],
                r["s_recv"].at[u, step],
                device("x", 0, 1),
            )
    for copy in loads[:2]:
        copy.wait()
    for which in range(2):
        for u in range(n):
            if which:
                for step in range(SIDE):
                    wait_all(r["rows"][u].at[1, pl.ds(0, PLANE_ROWS)], r["s_recv"].at[u, step])
            half = core if which == 0 else 1 - core
            depth = pl.ds(pl.multiple_of(offsets[u] + half * width[u], LANES), width[u])
            lhs = r["rows"][u][which, :, : width[u]]
            o = UNITS[u][0]
            for side, weight in enumerate((r["wg_v"], r["wu_v"])):
                part = jnp.dot(lhs, weight[depth, :], preferred_element_type=F32)
                columns = slice(side * 256, side * 256 + 256)
                first = which == 0 and all(UNITS[v][0] != o for v in range(u))
                r["acc"][o, :, columns] = part if first else r["acc"][o, :, columns] + part

    expert = node * 2 + local // 8
    lane = lax.broadcasted_iota(jnp.int32, (ROWS, LANES), 1)
    table = r["rows"][0][0, :, width[0] :]
    for o in range(3):
        here_table = jnp.dot(r["back"][o], table, preferred_element_type=F32)
        column = jnp.sum(jnp.where(lane == expert, here_table, 0.0), axis=1, keepdims=True)
        r["gcol"][o] = jnp.broadcast_to(column, (ROWS, LANES))

    total = r["acc"][0]
    for o in (1, 2):
        high = r["acc"][o].astype(BF16)
        low = (r["acc"][o] - high.astype(F32)).astype(BF16)
        total = total + jnp.dot(r["perm"][o - 1], high, preferred_element_type=F32)
        total = total + jnp.dot(r["perm"][o - 1], low, preferred_element_type=F32)
    gate_pre, up_pre = total[:, :256], total[:, 256:]
    hidden = (gate_pre * jax.nn.sigmoid(gate_pre) * up_pre).astype(BF16)
    for o in range(3):
        r["hid"][o] = jnp.dot(r["back"][o], hidden, preferred_element_type=F32).astype(BF16)
    loads[2].wait()

    def down(u, half):
        o = UNITS[u][0]
        columns = pl.ds(pl.multiple_of(offsets[u] + half * width[u], LANES), width[u])
        part = jnp.dot(r["hid"][o], r["wd_v"][:, columns], preferred_element_type=F32)
        return part * r["gcol"][o][:, :1]

    def second_block(u, ahead):
        second = lax.rem(here[axes(u)[1]] + ahead, SIDE)
        return pl.ds(pl.multiple_of(second * PLANE_ROWS, PLANE_ROWS), PLANE_ROWS)

    def third_block(u, ahead, step):
        second = lax.rem(here[axes(u)[1]] + ahead, SIDE)
        third = lax.rem(here[axes(u)[2]] + step, SIDE)
        return pl.ds(pl.multiple_of(second * PLANE_ROWS + third * LINE_ROWS, LINE_ROWS), LINE_ROWS)

    for u in range(n):
        r["sib_out"][u][...] = down(u, 1 - core).astype(BF16)
    for ahead in AHEAD:
        for u in range(n):
            at = second_block(u, ahead)
            send(r["sib_out"][u].at[at], r["sib_in"][u].at[at], r["r0_send"].at[u], r["r0_recv"].at[u, ahead], device("x", 0, 1))
    for u in range(n):
        r["own"][u][...] = down(u, core)
    for ahead in AHEAD:
        for u in range(n):
            at = second_block(u, ahead)
            wait_all(r["sib_in"][u].at[at], r["r0_recv"].at[u, ahead])
            r["r1_src"][u][at, :] = (r["own"][u][at, :] + r["sib_in"][u][at, :].astype(F32)).astype(BF16)
            for step in (2, 1, 3):
                send(
                    r["r1_src"][u].at[third_block(u, ahead, step)],
                    r["r1_dst"][u].at[ahead, step - 1],
                    r["r1_send"].at[u],
                    r["r1_recv"].at[u, ahead],
                    device(axes(u)[2], step, 0),
                )
    for u in range(n):
        wait_all(r["line"][u].at[pl.ds(0, 7)], r["p1_send"].at[u])
        wait_all(r["rows"][u].at[0, pl.ds(0, 3 * LINE_ROWS)], r["p2_send"].at[u])
        wait_all(r["rows"][u].at[0, pl.ds(0, 3 * PLANE_ROWS)], r["p3_send"].at[u])
        wait_all(r["rows"][u].at[0], r["s_send"].at[u])
    for ahead in AHEAD:
        for u in range(n):
            at = third_block(u, ahead, 0)
            wait_all(r["r1_dst"][u].at[ahead], r["r1_recv"].at[u, ahead])
            part = r["own"][u][at, :] + r["sib_in"][u][at, :].astype(F32)
            for step in range(3):
                part = part + r["r1_dst"][u][ahead, step].astype(F32)
            if ahead:
                r["r2_src"][u][ahead - 1] = part.astype(BF16)
                send(
                    r["r2_src"][u].at[ahead - 1],
                    r["r2_dst"][u].at[ahead - 1],
                    r["r2_send"].at[u],
                    r["r2_recv"].at[u],
                    device(axes(u)[1], ahead, 0),
                )
            else:
                r["r2_own"][u][...] = part
    for u in range(n):
        wait_all(r["r2_dst"][u], r["r2_recv"].at[u])
        part = r["r2_own"][u][...]
        for step in range(3):
            part = part + r["r2_dst"][u][step].astype(F32)
        for i in range(8):
            r["r3_src"][u][i] = part[2 * i : 2 * i + 2].astype(BF16)
        for step in (2, 1, 3, 0):
            first = lax.rem(here[axes(u)[0]] + step, SIDE)
            for flip in range(2):
                if step or flip:
                    send(
                        r["r3_src"][u].at[first * 2 + lax.rem(core + flip, 2)],
                        r["r3_dst"][u].at[core * SIDE + here[axes(u)[0]]],
                        r["r3_send"].at[u],
                        r["r3_recv"].at[u],
                        device(axes(u)[0], step, flip),
                    )
        r["r3_dst"][u][pl.ds(core * SIDE + here[axes(u)[0]], 1)] = r["r3_src"][u][pl.ds(line_slot(u), 1)]
    for u in range(n):
        wait_all(r["sib_out"][u], r["r0_send"].at[u])
        wait_all(r["r1_dst"][u], r["r1_send"].at[u])
        wait_all(r["r2_dst"][u], r["r2_send"].at[u])
        wait_all(r["r3_dst"][u].at[pl.ds(0, 7)], r["r3_send"].at[u])
    for u in range(n):
        wait_all(r["r3_dst"][u].at[pl.ds(0, 7)], r["r3_recv"].at[u])
        for h in range(2):
            part = r["r3_dst"][u][h * SIDE].astype(F32)
            for i in range(1, SIDE):
                part = part + r["r3_dst"][u][h * SIDE + i].astype(F32)
            out[:, pl.ds(offsets[u] + h * width[u], width[u])] = part.astype(BF16)


def layer(tokens, gates, node_set, w_gate, w_up, w_down):
    _, width = widths()
    n = len(UNITS)
    whole = [w + (LANES if u == 0 else 0) for u, w in enumerate(width)]
    dma = pltpu.SemaphoreType.DMA
    vmem = pltpu.VMEM
    depth, hidden = w_gate.shape
    scratch = dict(
        gates_v=vmem(gates.shape, BF16),
        set_v=vmem(node_set.shape, jnp.int32),
        wg_v=vmem(w_gate.shape, BF16),
        wu_v=vmem(w_up.shape, BF16),
        wd_v=vmem(w_down.shape, BF16),
        src=[vmem((2, TOK, w), BF16) for w in whole],
        line=[vmem((8, TOK, w), BF16) for w in whole],
        rows=[vmem((2, ROWS, w), BF16) for w in whole],
        acc=vmem((3, ROWS, 2 * hidden), F32),
        hid=vmem((3, ROWS, hidden), BF16),
        gcol=vmem((3, ROWS, LANES), F32),
        perm=vmem((2, ROWS, ROWS), BF16),
        back=vmem((3, ROWS, ROWS), BF16),
        sib_out=[vmem((ROWS, w), BF16) for w in width],
        sib_in=[vmem((ROWS, w), BF16) for w in width],
        r1_src=[vmem((ROWS, w), BF16) for w in width],
        own=[vmem((ROWS, w), F32) for w in width],
        r1_dst=[vmem((SIDE, 3, LINE_ROWS, w), BF16) for w in width],
        r2_src=[vmem((3, LINE_ROWS, w), BF16) for w in width],
        r2_own=[vmem((LINE_ROWS, w), F32) for w in width],
        r2_dst=[vmem((3, LINE_ROWS, w), BF16) for w in width],
        r3_src=[vmem((8, TOK, w), BF16) for w in width],
        r3_dst=[vmem((8, TOK, w), BF16) for w in width],
        load_sem=dma((3,)),
        tok_sem=dma((n, 2)),
        small_sem=dma((2,)),
        p1_send=dma((n,)),
        p1_recv=dma((n,)),
        p2_send=dma((n,)),
        p2_recv=dma((n, 3)),
        p3_send=dma((n,)),
        p3_recv=dma((n, 3)),
        s_send=dma((n,)),
        s_recv=dma((n, 4)),
        r0_send=dma((n,)),
        r0_recv=dma((n, SIDE)),
        r1_send=dma((n,)),
        r1_recv=dma((n, SIDE)),
        r2_send=dma((n,)),
        r2_recv=dma((n,)),
        r3_send=dma((n,)),
        r3_recv=dma((n,)),
    )
    return pl.pallas_call(
        kernel,
        out_shape=jax.ShapeDtypeStruct(tokens.shape, BF16),
        in_specs=[pl.BlockSpec(memory_space=pl.ANY)] * 6,
        out_specs=pl.BlockSpec(memory_space=pltpu.VMEM),
        scratch_shapes=scratch,
        compiler_params=pltpu.CompilerParams(
            collective_id=0, has_side_effects=True, vmem_limit_bytes=64 << 20
        ),
    )(tokens, gates, node_set, w_gate, w_up, w_down)


def solution(mesh):
    rows, columns = P(("node", "local"), None), P(None, ("node", "local"))
    return jax.shard_map(
        layer,
        mesh=mesh,
        in_specs=(rows, rows, rows, columns, columns, rows),
        out_specs=rows,
        check_vma=False,
    )
```

```python
import functools

import jax
import jax.numpy as jnp
from jax import lax
from jax.experimental import pallas as pl
from jax.experimental.pallas import tpu as pltpu
from jax.sharding import PartitionSpec as P

MESH = pl.DeviceIdType.MESH
SIDE = 4
ROWS = 256
TOK = 2
LINE_ROWS = 16
PLANE_ROWS = 64
LANES = 128
AHEAD = (2, 1, 3, 0)
ORDERS = ("xyz", "yzx", "zxy")
UNITS = ((0, 9), (1, 10), (2, 9))
GATED = 0
F32, BF16 = jnp.float32, jnp.bfloat16


def widths():
    offsets, start = [], 0
    for _, blocks in UNITS:
        offsets.append(start)
        start += 2 * blocks * LANES
    return offsets, [blocks * LANES for _, blocks in UNITS]


def row_of(order, at):
    place = dict(x=(at >> 2) & 3, z=(at >> 4) & 3, y=(at >> 6) & 3)
    first, second, third = (place[axis] for axis in ORDERS[order])
    return (((second * SIDE + third) * SIDE + first) << 2) + (at & 3)


def kernel(tok, gates, node_set, wg, wu, wd, out, **r):
    offsets, width = widths()
    n = len(UNITS)

    node, local = lax.axis_index("node"), lax.axis_index("local")
    here = dict(x=local // SIDE, y=local % SIDE, z=node // 2)
    core = node % 2

    def device(axis, step, flip):
        at = dict(here)
        at[axis] = lax.rem(at[axis] + step, SIDE)
        other = lax.rem(core + flip, 2)
        return (at["z"] * 2 + other, at["x"] * SIDE + at["y"])

    loads = [
        pltpu.make_async_copy(wg, r["wg_v"], r["load_sem"].at[0]),
        pltpu.make_async_copy(wu, r["wu_v"], r["load_sem"].at[1]),
        pltpu.make_async_copy(wd, r["wd_v"], r["load_sem"].at[2]),
    ]
    small = [
        pltpu.make_async_copy(gates, r["gates_v"], r["small_sem"].at[0]),
        pltpu.make_async_copy(node_set, r["set_v"], r["small_sem"].at[1]),
    ]
    own = []
    for u in range(n):
        for h in range(2):
            own.append(
                pltpu.make_async_copy(
                    tok.at[:, pl.ds(offsets[u] + h * width[u], width[u])],
                    r["src"][u].at[h, :, pl.ds(0, width[u])],
                    r["tok_sem"].at[u, h],
                )
            )
    for copy in small + own:
        copy.start()

    barrier = pltpu.get_barrier_semaphore()
    partners = [(axis, step, flip) for axis in "xyz" for step in range(1, SIDE) for flip in range(2)]
    partners.append(("x", 0, 1))
    for partner in partners:
        pl.semaphore_signal(barrier, inc=1, device_id=device(*partner), device_id_type=MESH)
    for copy in small:
        copy.wait()
    lane = lax.broadcasted_iota(jnp.int32, (TOK, LANES), 1)
    table = jnp.zeros((TOK, LANES), F32)
    gate_v, set_v = r["gates_v"][...].astype(F32), r["set_v"][...]
    for j in range(set_v.shape[1]):
        pair = jnp.where(lane % 2 == 0, gate_v[:, 2 * j : 2 * j + 1], gate_v[:, 2 * j + 1 : 2 * j + 2])
        table = table + jnp.where(set_v[:, j : j + 1] == lane // 2, pair, 0.0)
    for h in range(2):
        r["src"][GATED][h, :, width[GATED] :] = table.astype(BF16)
    for copy in own:
        copy.wait()
    pl.semaphore_wait(barrier, len(partners))


    def send(src, dst, send_sem, recv_sem, to):
        copy = pltpu.make_async_remote_copy(
            src_ref=src, dst_ref=dst, send_sem=send_sem, recv_sem=recv_sem, device_id=to, device_id_type=MESH
        )
        copy.start()

    def axes(u):
        return ORDERS[UNITS[u][0]]

    def line_slot(u):
        return here[axes(u)[0]] * 2 + core

    for u in range(n):
        for step in (1, 3, 2, 0):
            for flip in range(2):
                if step or flip:
                    send(
                        r["src"][u].at[lax.rem(core + flip, 2)],
                        r["line"][u].at[line_slot(u)],
                        r["p1_send"].at[u],
                        r["p1_recv"].at[u],
                        device(axes(u)[0], step, flip),
                    )
        r["line"][u][pl.ds(line_slot(u), 1)] = r["src"][u][pl.ds(core, 1)]

    def wait_all(ref, sem):
        pltpu.make_async_copy(ref, ref, sem).wait()

    for copy in loads:
        copy.start()
    down_at = lax.broadcasted_iota(jnp.int32, (ROWS, ROWS), 0)
    across = lax.broadcasted_iota(jnp.int32, (ROWS, ROWS), 1)
    for o in (1, 2):
        r["perm"][o - 1] = (row_of(o, down_at) == across).astype(F32).astype(BF16)
        r["back"][o - 1] = (row_of(o, across) == down_at).astype(F32).astype(BF16)
    def second_block(u, ahead):
        second = lax.rem(here[axes(u)[1]] + ahead, SIDE)
        return pl.ds(pl.multiple_of(second * PLANE_ROWS, PLANE_ROWS), PLANE_ROWS)

    def third_block(u, ahead, step):
        second = lax.rem(here[axes(u)[1]] + ahead, SIDE)
        third = lax.rem(here[axes(u)[2]] + step, SIDE)
        return pl.ds(pl.multiple_of(second * PLANE_ROWS + third * LINE_ROWS, LINE_ROWS), LINE_ROWS)

    def gather3(u, back):
        view = r["rows"][u].at[0, third_block(u, SIDE - back, 0)]
        for step in (2, 1, 3):
            send(view, view, r["p3_send"].at[u], r["p3_recv"].at[u, back], device(axes(u)[2], step, 0))

    for u in range(n):
        wait_all(r["line"][u].at[pl.ds(0, 7)], r["p1_recv"].at[u])
        block = jnp.concatenate([r["line"][u][i].astype(F32) for i in range(8)], axis=0)
        view = r["rows"][u].at[0, third_block(u, 0, 0)]
        view[...] = block.astype(BF16)
        for step in (2, 1, 3):
            send(view, view, r["p2_send"].at[u], r["p2_recv"].at[u, step - 1], device(axes(u)[1], step, 0))
    for u in range(n):
        gather3(u, 0)
    for back in (1, 3, 2):
        for u in range(n):
            wait_all(r["rows"][u].at[0, pl.ds(0, LINE_ROWS)], r["p2_recv"].at[u, back - 1])
            gather3(u, back)
    for back in (0, 1, 3, 2):
        for u in range(n):
            wait_all(r["rows"][u].at[0, pl.ds(0, 3 * LINE_ROWS)], r["p3_recv"].at[u, back])
            at = second_block(u, SIDE - back)
            send(
                r["rows"][u].at[0, at],
                r["rows"][u].at[1, at],
                r["s_send"].at[u],
                r["s_recv"].at[u, back],
                device("x", 0, 1),
            )
    for copy in loads[:2]:
        copy.wait()
    for which in range(2):
        for u in range(n):
            if which:
                for step in range(SIDE):
                    wait_all(r["rows"][u].at[1, pl.ds(0, PLANE_ROWS)], r["s_recv"].at[u, step])
            half = core if which == 0 else 1 - core
            depth = pl.ds(pl.multiple_of(offsets[u] + half * width[u], LANES), width[u])
            lhs = r["rows"][u][which, :, : width[u]]
            o = UNITS[u][0]
            for side, weight in enumerate((r["wg_v"], r["wu_v"])):
                part = jnp.dot(lhs, weight[depth, :], preferred_element_type=F32)
                columns = slice(side * 256, side * 256 + 256)
                first = which == 0 and all(UNITS[v][0] != o for v in range(u))
                r["acc"][o, :, columns] = part if first else r["acc"][o, :, columns] + part

    expert = node * 2 + local // 8
    lane = lax.broadcasted_iota(jnp.int32, (ROWS, LANES), 1)
    table = r["rows"][GATED][0, :, width[GATED] :]
    for o in range(3):
        here_table = table if o == 0 else jnp.dot(r["back"][o - 1], table, preferred_element_type=F32)
        column = jnp.sum(jnp.where(lane == expert, here_table.astype(F32), 0.0), axis=1, keepdims=True)
        r["gcol"][o] = jnp.broadcast_to(column, (ROWS, LANES))

    total = r["acc"][0]
    for o in (1, 2):
        high = r["acc"][o].astype(BF16)
        low = (r["acc"][o] - high.astype(F32)).astype(BF16)
        total = total + jnp.dot(r["perm"][o - 1], high, preferred_element_type=F32)
        total = total + jnp.dot(r["perm"][o - 1], low, preferred_element_type=F32)
    gate_pre, up_pre = total[:, :256], total[:, 256:]
    hidden = (gate_pre * jax.nn.sigmoid(gate_pre) * up_pre).astype(BF16)
    r["hid"][0] = hidden
    for o in (1, 2):
        r["hid"][o] = jnp.dot(r["back"][o - 1], hidden, preferred_element_type=F32).astype(BF16)
    loads[2].wait()

    def down(u, half):
        o = UNITS[u][0]
        columns = pl.ds(pl.multiple_of(offsets[u] + half * width[u], LANES), width[u])
        part = jnp.dot(r["hid"][o], r["wd_v"][:, columns], preferred_element_type=F32)
        return part * jnp.concatenate([r["gcol"][o]] * UNITS[u][1], axis=1)

    def reduce0(u, ahead):
        at = second_block(u, ahead)
        send(r["sib_out"][u].at[at], r["sib_in"][u].at[at], r["r0_send"].at[u], r["r0_recv"].at[u, ahead], device("x", 0, 1))

    for u in range(n):
        r["sib_out"][u][...] = down(u, 1 - core).astype(BF16)
        reduce0(u, AHEAD[0])
    for ahead in AHEAD[1:]:
        for u in range(n):
            reduce0(u, ahead)

    def reduce1(u, ahead):
        at = second_block(u, ahead)
        wait_all(r["sib_in"][u].at[at], r["r0_recv"].at[u, ahead])
        r["r1_src"][u][at, :] = (r["own"][u][at, :] + r["sib_in"][u][at, :].astype(F32)).astype(BF16)
        for step in (2, 1, 3):
            send(
                r["r1_src"][u].at[third_block(u, ahead, step)],
                r["r1_dst"][u].at[ahead, step - 1],
                r["r1_send"].at[u],
                r["r1_recv"].at[u, ahead],
                device(axes(u)[2], step, 0),
            )

    for u in range(n):
        r["own"][u][...] = down(u, core)
        reduce1(u, AHEAD[0])
    for ahead in AHEAD[1:]:
        for u in range(n):
            reduce1(u, ahead)
    for u in range(n):
        wait_all(r["line"][u].at[pl.ds(0, 7)], r["p1_send"].at[u])
        wait_all(r["rows"][u].at[0, pl.ds(0, 3 * LINE_ROWS)], r["p2_send"].at[u])
        wait_all(r["rows"][u].at[0, pl.ds(0, 3 * PLANE_ROWS)], r["p3_send"].at[u])
        wait_all(r["rows"][u].at[0], r["s_send"].at[u])
    for ahead in AHEAD:
        for u in range(n):
            at = third_block(u, ahead, 0)
            wait_all(r["r1_dst"][u].at[ahead], r["r1_recv"].at[u, ahead])
            part = r["own"][u][at, :] + r["sib_in"][u][at, :].astype(F32)
            for step in range(3):
                part = part + r["r1_dst"][u][ahead, step].astype(F32)
            if ahead:
                r["r2_src"][u][ahead - 1] = part.astype(BF16)
                send(
                    r["r2_src"][u].at[ahead - 1],
                    r["r2_dst"][u].at[ahead - 1],
                    r["r2_send"].at[u],
                    r["r2_recv"].at[u],
                    device(axes(u)[1], ahead, 0),
                )
            else:
                r["r2_own"][u][...] = part
    for u in range(n):
        wait_all(r["r2_dst"][u], r["r2_recv"].at[u])
        part = r["r2_own"][u][...]
        for step in range(3):
            part = part + r["r2_dst"][u][step].astype(F32)
        for i in range(8):
            r["r3_src"][u][i] = part[2 * i : 2 * i + 2].astype(BF16)
        for step in (2, 1, 3, 0):
            first = lax.rem(here[axes(u)[0]] + step, SIDE)
            for flip in range(2):
                if step or flip:
                    send(
                        r["r3_src"][u].at[first * 2 + lax.rem(core + flip, 2)],
                        r["r3_dst"][u].at[core * SIDE + here[axes(u)[0]]],
                        r["r3_send"].at[u],
                        r["r3_recv"].at[u],
                        device(axes(u)[0], step, flip),
                    )
        r["r3_dst"][u][pl.ds(core * SIDE + here[axes(u)[0]], 1)] = r["r3_src"][u][pl.ds(line_slot(u), 1)]
    for u in range(n):
        wait_all(r["sib_out"][u], r["r0_send"].at[u])
        wait_all(r["r1_dst"][u], r["r1_send"].at[u])
        wait_all(r["r2_dst"][u], r["r2_send"].at[u])
        wait_all(r["r3_dst"][u].at[pl.ds(0, 7)], r["r3_send"].at[u])
    for u in range(n):
        wait_all(r["r3_dst"][u].at[pl.ds(0, 7)], r["r3_recv"].at[u])
        for h in range(2):
            part = r["r3_dst"][u][h * SIDE].astype(F32)
            for i in range(1, SIDE):
                part = part + r["r3_dst"][u][h * SIDE + i].astype(F32)
            out[:, pl.ds(offsets[u] + h * width[u], width[u])] = part.astype(BF16)


def layer(tokens, gates, node_set, w_gate, w_up, w_down):
    _, width = widths()
    n = len(UNITS)
    whole = [w + (LANES if u == GATED else 0) for u, w in enumerate(width)]
    dma = pltpu.SemaphoreType.DMA
    vmem = pltpu.VMEM
    depth, hidden = w_gate.shape
    scratch = dict(
        gates_v=vmem(gates.shape, BF16),
        set_v=vmem(node_set.shape, jnp.int32),
        wg_v=vmem(w_gate.shape, BF16),
        wu_v=vmem(w_up.shape, BF16),
        wd_v=vmem(w_down.shape, BF16),
        src=[vmem((2, TOK, w), BF16) for w in whole],
        line=[vmem((8, TOK, w), BF16) for w in whole],
        rows=[vmem((2, ROWS, w), BF16) for w in whole],
        acc=vmem((3, ROWS, 2 * hidden), F32),
        hid=vmem((3, ROWS, hidden), BF16),
        gcol=vmem((3, ROWS, LANES), F32),
        perm=vmem((2, ROWS, ROWS), BF16),
        back=vmem((2, ROWS, ROWS), BF16),
        sib_out=[vmem((ROWS, w), BF16) for w in width],
        sib_in=[vmem((ROWS, w), BF16) for w in width],
        r1_src=[vmem((ROWS, w), BF16) for w in width],
        own=[vmem((ROWS, w), F32) for w in width],
        r1_dst=[vmem((SIDE, 3, LINE_ROWS, w), BF16) for w in width],
        r2_src=[vmem((3, LINE_ROWS, w), BF16) for w in width],
        r2_own=[vmem((LINE_ROWS, w), F32) for w in width],
        r2_dst=[vmem((3, LINE_ROWS, w), BF16) for w in width],
        r3_src=[vmem((8, TOK, w), BF16) for w in width],
        r3_dst=[vmem((8, TOK, w), BF16) for w in width],
        load_sem=dma((3,)),
        tok_sem=dma((n, 2)),
        small_sem=dma((2,)),
        p1_send=dma((n,)),
        p1_recv=dma((n,)),
        p2_send=dma((n,)),
        p2_recv=dma((n, 3)),
        p3_send=dma((n,)),
        p3_recv=dma((n, SIDE)),
        s_send=dma((n,)),
        s_recv=dma((n, SIDE)),
        r0_send=dma((n,)),
        r0_recv=dma((n, SIDE)),
        r1_send=dma((n,)),
        r1_recv=dma((n, SIDE)),
        r2_send=dma((n,)),
        r2_recv=dma((n,)),
        r3_send=dma((n,)),
        r3_recv=dma((n,)),
    )
    return pl.pallas_call(
        kernel,
        out_shape=jax.ShapeDtypeStruct(tokens.shape, BF16),
        in_specs=[pl.BlockSpec(memory_space=pl.ANY)] * 6,
        out_specs=pl.BlockSpec(memory_space=pltpu.VMEM),
        scratch_shapes=scratch,
        compiler_params=pltpu.CompilerParams(
            collective_id=0, has_side_effects=True, vmem_limit_bytes=48 << 20
        ),
    )(*[pltpu.with_memory_space_constraint(a, pltpu.HBM) for a in (tokens, gates, node_set, w_gate, w_up, w_down)])


def solution(mesh):
    rows, columns = P(("node", "local"), None), P(None, ("node", "local"))
    return jax.shard_map(
        layer,
        mesh=mesh,
        in_specs=(rows, rows, rows, columns, columns, rows),
        out_specs=rows,
        check_vma=False,
    )
```

```python
import functools

import jax
import jax.numpy as jnp
from jax import lax
from jax.experimental import pallas as pl
from jax.experimental.pallas import tpu as pltpu
from jax.sharding import PartitionSpec as P

MESH = pl.DeviceIdType.MESH
SIDE = 4
ROWS = 256
TOK = 2
LINE_ROWS = 16
PLANE_ROWS = 64
LANES = 128
TURNS = dict(
    x=((0, 2, 1, 3), (0, 3, 2, 1), (0, 3, 1, 2), (0, 1, 2, 3)),
    y=((1, 2, 3, 0), (1, 3, 0, 2), (1, 0, 3, 2), (1, 0, 2, 3)),
    z=((2, 1, 3, 0), (3, 2, 0, 1), (0, 3, 1, 2), (1, 0, 2, 3)),
)
ORDERS = ("xyz", "yzx", "zxy")
UNITS = ((0, 9), (1, 10), (2, 9))
GATED = 0
F32, BF16 = jnp.float32, jnp.bfloat16


def widths():
    offsets, start = [], 0
    for _, blocks in UNITS:
        offsets.append(start)
        start += 2 * blocks * LANES
    return offsets, [blocks * LANES for _, blocks in UNITS]


def row_of(order, at):
    place = dict(x=(at >> 2) & 3, z=(at >> 4) & 3, y=(at >> 6) & 3)
    first, second, third = (place[axis] for axis in ORDERS[order])
    return (((second * SIDE + third) * SIDE + first) << 2) + (at & 3)


def kernel(tok, gates, node_set, wg, wu, wd, out, **r):
    offsets, width = widths()
    n = len(UNITS)

    node, local = lax.axis_index("node"), lax.axis_index("local")
    here = dict(x=local // SIDE, y=local % SIDE, z=node // 2)
    core = node % 2

    def device(axis, step, flip):
        at = dict(here)
        at[axis] = lax.rem(at[axis] + step, SIDE)
        other = lax.rem(core + flip, 2)
        return (at["z"] * 2 + other, at["x"] * SIDE + at["y"])

    depth_at = [sum(width[:u]) for u in range(n)]
    loads = [
        pltpu.make_async_copy(wg, r["wg_v"], r["load_sem"].at[0]),
        pltpu.make_async_copy(wu, r["wu_v"], r["load_sem"].at[1]),
    ]
    for u in range(n):
        mine = pl.ds(pl.multiple_of(offsets[u] + core * width[u], LANES), width[u])
        there = pl.ds(depth_at[u], width[u])
        loads.append(pltpu.make_async_copy(wd.at[:, mine], r["w2"].at[0, :, there], r["load_sem"].at[2]))
    small = [
        pltpu.make_async_copy(gates, r["gates_v"], r["small_sem"].at[0]),
        pltpu.make_async_copy(node_set, r["set_v"], r["small_sem"].at[1]),
    ]
    own = []
    for u in range(n):
        for h in range(2):
            own.append(
                pltpu.make_async_copy(
                    tok.at[:, pl.ds(offsets[u] + h * width[u], width[u])],
                    r["src"][u].at[h, :, pl.ds(0, width[u])],
                    r["tok_sem"].at[u, h],
                )
            )
    for copy in small + own:
        copy.start()

    barrier = pltpu.get_barrier_semaphore()
    partners = [(axis, step, flip) for axis in "xyz" for step in range(1, SIDE) for flip in range(2)]
    partners.append(("x", 0, 1))
    for partner in partners:
        pl.semaphore_signal(barrier, inc=1, device_id=device(*partner), device_id_type=MESH)
    for copy in small:
        copy.wait()
    lane = lax.broadcasted_iota(jnp.int32, (TOK, LANES), 1)
    table = jnp.zeros((TOK, LANES), F32)
    gate_v, set_v = r["gates_v"][...].astype(F32), r["set_v"][...]
    for j in range(set_v.shape[1]):
        pair = jnp.where(lane % 2 == 0, gate_v[:, 2 * j : 2 * j + 1], gate_v[:, 2 * j + 1 : 2 * j + 2])
        table = table + jnp.where(set_v[:, j : j + 1] == lane // 2, pair, 0.0)
    for h in range(2):
        r["src"][GATED][h, :, width[GATED] :] = table.astype(BF16)
    for copy in own:
        copy.wait()
    pl.semaphore_wait(barrier, len(partners))


    def send(src, dst, send_sem, recv_sem, to):
        copy = pltpu.make_async_remote_copy(
            src_ref=src, dst_ref=dst, send_sem=send_sem, recv_sem=recv_sem, device_id=to, device_id_type=MESH
        )
        copy.start()

    def axes(u):
        return ORDERS[UNITS[u][0]]

    def line_slot(u):
        return here[axes(u)[0]] * 2 + core

    for u in range(n):
        for step in (1, 3, 2, 0):
            for flip in range(2):
                if step or flip:
                    send(
                        r["src"][u].at[lax.rem(core + flip, 2)],
                        r["line"][u].at[line_slot(u)],
                        r["p1_send"].at[u],
                        r["p1_recv"].at[u],
                        device(axes(u)[0], step, flip),
                    )
        r["line"][u][pl.ds(line_slot(u), 1)] = r["src"][u][pl.ds(core, 1)]

    def wait_all(ref, sem):
        pltpu.make_async_copy(ref, ref, sem).wait()

    for copy in loads:
        copy.start()
    for u in range(n):
        other = pl.ds(pl.multiple_of(offsets[u] + (1 - core) * width[u], LANES), width[u])
        there = pl.ds(depth_at[u], width[u])
        send(wd.at[:, other], r["w2"].at[1, :, there], r["w_send"], r["w_recv"], device("x", 0, 1))
    down_at = lax.broadcasted_iota(jnp.int32, (ROWS, ROWS), 0)
    across = lax.broadcasted_iota(jnp.int32, (ROWS, ROWS), 1)
    for o in (1, 2):
        r["perm"][o - 1] = (row_of(o, down_at) == across).astype(F32).astype(BF16)
        r["back"][o - 1] = (row_of(o, across) == down_at).astype(F32).astype(BF16)
    def second_block(u, ahead):
        second = lax.rem(here[axes(u)[1]] + ahead, SIDE)
        return pl.ds(pl.multiple_of(second * PLANE_ROWS, PLANE_ROWS), PLANE_ROWS)

    def third_block(u, ahead, step):
        second = lax.rem(here[axes(u)[1]] + ahead, SIDE)
        third = lax.rem(here[axes(u)[2]] + step, SIDE)
        return pl.ds(pl.multiple_of(second * PLANE_ROWS + third * LINE_ROWS, LINE_ROWS), LINE_ROWS)

    def gather3(u, back):
        view = r["rows"][u].at[0, third_block(u, SIDE - back, 0)]
        for step in (2, 1, 3):
            send(view, view, r["p3_send"].at[u], r["p3_recv"].at[u, back], device(axes(u)[2], step, 0))

    for u in range(n):
        wait_all(r["line"][u].at[pl.ds(0, 7)], r["p1_recv"].at[u])
        block = jnp.concatenate([r["line"][u][i].astype(F32) for i in range(8)], axis=0)
        view = r["rows"][u].at[0, third_block(u, 0, 0)]
        view[...] = block.astype(BF16)
        for step in (2, 1, 3):
            send(view, view, r["p2_send"].at[u], r["p2_recv"].at[u, step - 1], device(axes(u)[1], step, 0))
    for u in range(n):
        gather3(u, 0)
    for back in (1, 3, 2):
        for u in range(n):
            wait_all(r["rows"][u].at[0, pl.ds(0, LINE_ROWS)], r["p2_recv"].at[u, back - 1])
            gather3(u, back)
    for back in (0, 1, 3, 2):
        for u in range(n):
            wait_all(r["rows"][u].at[0, pl.ds(0, 3 * LINE_ROWS)], r["p3_recv"].at[u, back])
            at = second_block(u, SIDE - back)
            send(
                r["rows"][u].at[0, at],
                r["rows"][u].at[1, at],
                r["s_send"].at[u],
                r["s_recv"].at[u, back],
                device("x", 0, 1),
            )
    for copy in loads[:2]:
        copy.wait()
    for which in range(2):
        for u in range(n):
            if which:
                for step in range(SIDE):
                    wait_all(r["rows"][u].at[1, pl.ds(0, PLANE_ROWS)], r["s_recv"].at[u, step])
            half = core if which == 0 else 1 - core
            depth = pl.ds(pl.multiple_of(offsets[u] + half * width[u], LANES), width[u])
            lhs = r["rows"][u][which, :, : width[u]]
            o = UNITS[u][0]
            for side, weight in enumerate((r["wg_v"], r["wu_v"])):
                part = jnp.dot(lhs, weight[depth, :], preferred_element_type=F32)
                columns = slice(side * 256, side * 256 + 256)
                first = which == 0 and all(UNITS[v][0] != o for v in range(u))
                r["acc"][o, :, columns] = part if first else r["acc"][o, :, columns] + part

    lane = lax.broadcasted_iota(jnp.int32, (ROWS, LANES), 1)
    table = r["rows"][GATED][0, :, width[GATED] :]
    for o in range(3):
        here_table = table if o == 0 else jnp.dot(r["back"][o - 1], table, preferred_element_type=F32)
        for who in range(2):
            expert = (here["z"] * 2 + lax.rem(core + who, 2)) * 2 + local // 8
            column = jnp.sum(jnp.where(lane == expert, here_table.astype(F32), 0.0), axis=1, keepdims=True)
            r["gcol"][who, o] = jnp.broadcast_to(column, (ROWS, LANES))

    total = r["acc"][0]
    for o in (1, 2):
        high = r["acc"][o].astype(BF16)
        low = (r["acc"][o] - high.astype(F32)).astype(BF16)
        total = total + jnp.dot(r["perm"][o - 1], high, preferred_element_type=F32)
        total = total + jnp.dot(r["perm"][o - 1], low, preferred_element_type=F32)
    gate_pre, up_pre = total[:, :256], total[:, 256:]
    hidden = (gate_pre * jax.nn.sigmoid(gate_pre) * up_pre).astype(BF16)
    r["hid"][0, 0] = hidden
    send(r["hid"].at[0, 0], r["hid"].at[1, 0], r["h_send"], r["h_recv"], device("x", 0, 1))

    def down(u, who):
        o = UNITS[u][0]
        weight = r["w2"][who, :, depth_at[u] : depth_at[u] + width[u]]
        part = jnp.dot(r["hid"][who, o], weight, preferred_element_type=F32)
        return part * jnp.concatenate([r["gcol"][who, o]] * UNITS[u][1], axis=1)

    def reorder(who):
        for o in (1, 2):
            r["hid"][who, o] = jnp.dot(r["back"][o - 1], r["hid"][who, 0], preferred_element_type=F32).astype(BF16)

    reorder(0)
    wait_all(r["w2"].at[0], r["load_sem"].at[2])
    wait_all(r["w2"].at[1], r["w_recv"])
    for u in range(n):
        r["own"][u][...] = down(u, 0)
    wait_all(r["hid"].at[1, 0], r["h_recv"])
    reorder(1)
    def turn(u, slot):
        axis = axes(u)[1]
        place = TURNS[axis][0][slot]
        for i in range(1, SIDE):
            place = jnp.where(here[axis] == i, TURNS[axis][i][slot], place)
        return place

    def third_rows(u, place, step):
        third = lax.rem(here[axes(u)[2]] + step, SIDE)
        return pl.ds(pl.multiple_of(place * PLANE_ROWS + third * LINE_ROWS, LINE_ROWS), LINE_ROWS)

    for u in range(n):
        total = r["own"][u][...] + down(u, 1)
        r["own"][u][...] = total
        r["r1_src"][u][...] = total.astype(BF16)
        for slot in range(SIDE):
            for step in (2, 1, 3):
                send(
                    r["r1_src"][u].at[third_rows(u, turn(u, slot), step)],
                    r["r1_dst"][u].at[slot, step - 1],
                    r["r1_send"].at[u],
                    r["r1_recv"].at[u, slot],
                    device(axes(u)[2], step, 0),
                )
    for u in range(n):
        wait_all(r["line"][u].at[pl.ds(0, 7)], r["p1_send"].at[u])
        wait_all(r["rows"][u].at[0, pl.ds(0, 3 * LINE_ROWS)], r["p2_send"].at[u])
        wait_all(r["rows"][u].at[0, pl.ds(0, 3 * PLANE_ROWS)], r["p3_send"].at[u])
        wait_all(r["rows"][u].at[0], r["s_send"].at[u])
    wait_all(r["w2"].at[1], r["w_send"])
    wait_all(r["hid"].at[0, 0], r["h_send"])
    def reduce2(u, slot):
        place = turn(u, slot)
        wait_all(r["r1_dst"][u].at[slot], r["r1_recv"].at[u, slot])
        part = r["own"][u][third_rows(u, place, 0), :]
        for step in range(3):
            part = part + r["r1_dst"][u][slot, step].astype(F32)
        ahead = lax.rem(place + SIDE - here[axes(u)[1]], SIDE)

        @pl.when(ahead == 0)
        def _():
            r["r2_own"][u][...] = part

        @pl.when(ahead != 0)
        def _():
            r["r2_src"][u][slot] = part.astype(BF16)
            send(
                r["r2_src"][u].at[slot],
                r["r2_dst"][u].at[ahead - 1],
                r["r2_send"].at[u],
                r["r2_recv"].at[u],
                device(axes(u)[1], ahead, 0),
            )

    for slot in range(SIDE):
        for u in range(n):
            reduce2(u, slot)
    def reduce3(u):
        wait_all(r["r2_dst"][u], r["r2_recv"].at[u])
        part = r["r2_own"][u][...]
        for step in range(3):
            part = part + r["r2_dst"][u][step].astype(F32)
        for i in range(8):
            r["r3_src"][u][i] = part[2 * i : 2 * i + 2].astype(BF16)
        for step in (2, 1, 3, 0):
            first = lax.rem(here[axes(u)[0]] + step, SIDE)
            for flip in range(2):
                if step or flip:
                    send(
                        r["r3_src"][u].at[first * 2 + lax.rem(core + flip, 2)],
                        r["r3_dst"][u].at[core * SIDE + here[axes(u)[0]]],
                        r["r3_send"].at[u],
                        r["r3_recv"].at[u],
                        device(axes(u)[0], step, flip),
                    )
        r["r3_dst"][u][pl.ds(core * SIDE + here[axes(u)[0]], 1)] = r["r3_src"][u][pl.ds(line_slot(u), 1)]

    for u in range(n):
        pl.when(here[axes(u)[1]] == TURNS[axes(u)[1]][0][0])(functools.partial(reduce3, u))
    for u in range(n):
        pl.when(here[axes(u)[1]] != TURNS[axes(u)[1]][0][0])(functools.partial(reduce3, u))
    for u in range(n):
        wait_all(r["r1_dst"][u], r["r1_send"].at[u])
        wait_all(r["r2_dst"][u], r["r2_send"].at[u])
        wait_all(r["r3_dst"][u].at[pl.ds(0, 7)], r["r3_send"].at[u])
    for u in range(n):
        wait_all(r["r3_dst"][u].at[pl.ds(0, 7)], r["r3_recv"].at[u])
        for h in range(2):
            part = r["r3_dst"][u][h * SIDE].astype(F32)
            for i in range(1, SIDE):
                part = part + r["r3_dst"][u][h * SIDE + i].astype(F32)
            out[:, pl.ds(offsets[u] + h * width[u], width[u])] = part.astype(BF16)


def layer(tokens, gates, node_set, w_gate, w_up, w_down):
    _, width = widths()
    n = len(UNITS)
    whole = [w + (LANES if u == GATED else 0) for u, w in enumerate(width)]
    dma = pltpu.SemaphoreType.DMA
    vmem = pltpu.VMEM
    depth, hidden = w_gate.shape
    scratch = dict(
        gates_v=vmem(gates.shape, BF16),
        set_v=vmem(node_set.shape, jnp.int32),
        wg_v=vmem(w_gate.shape, BF16),
        wu_v=vmem(w_up.shape, BF16),
        w2=vmem((2, hidden, depth // 2), BF16),
        src=[vmem((2, TOK, w), BF16) for w in whole],
        line=[vmem((8, TOK, w), BF16) for w in whole],
        rows=[vmem((2, ROWS, w), BF16) for w in whole],
        acc=vmem((3, ROWS, 2 * hidden), F32),
        hid=vmem((2, 3, ROWS, hidden), BF16),
        gcol=vmem((2, 3, ROWS, LANES), F32),
        perm=vmem((2, ROWS, ROWS), BF16),
        back=vmem((2, ROWS, ROWS), BF16),
        r1_src=[vmem((ROWS, w), BF16) for w in width],
        own=[vmem((ROWS, w), F32) for w in width],
        r1_dst=[vmem((SIDE, 3, LINE_ROWS, w), BF16) for w in width],
        r2_src=[vmem((SIDE, LINE_ROWS, w), BF16) for w in width],
        r2_own=[vmem((LINE_ROWS, w), F32) for w in width],
        r2_dst=[vmem((3, LINE_ROWS, w), BF16) for w in width],
        r3_src=[vmem((8, TOK, w), BF16) for w in width],
        r3_dst=[vmem((8, TOK, w), BF16) for w in width],
        load_sem=dma((3,)),
        tok_sem=dma((n, 2)),
        small_sem=dma((2,)),
        p1_send=dma((n,)),
        p1_recv=dma((n,)),
        p2_send=dma((n,)),
        p2_recv=dma((n, 3)),
        p3_send=dma((n,)),
        p3_recv=dma((n, SIDE)),
        s_send=dma((n,)),
        s_recv=dma((n, SIDE)),
        w_send=dma,
        w_recv=dma,
        h_send=dma,
        h_recv=dma,
        r1_send=dma((n,)),
        r1_recv=dma((n, SIDE)),
        r2_send=dma((n,)),
        r2_recv=dma((n,)),
        r3_send=dma((n,)),
        r3_recv=dma((n,)),
    )
    return pl.pallas_call(
        kernel,
        out_shape=jax.ShapeDtypeStruct(tokens.shape, BF16),
        in_specs=[pl.BlockSpec(memory_space=pl.ANY)] * 6,
        out_specs=pl.BlockSpec(memory_space=pltpu.VMEM),
        scratch_shapes=scratch,
        compiler_params=pltpu.CompilerParams(
            collective_id=0, has_side_effects=True, vmem_limit_bytes=48 << 20
        ),
    )(*[pltpu.with_memory_space_constraint(a, pltpu.HBM) for a in (tokens, gates, node_set, w_gate, w_up, w_down)])


def solution(mesh):
    rows, columns = P(("node", "local"), None), P(None, ("node", "local"))
    return jax.shard_map(
        layer,
        mesh=mesh,
        in_specs=(rows, rows, rows, columns, columns, rows),
        out_specs=rows,
        check_vma=False,
    )
```

```python
import functools

import jax
import jax.numpy as jnp
from jax import lax
from jax.experimental import pallas as pl
from jax.experimental.pallas import tpu as pltpu
from jax.sharding import PartitionSpec as P

MESH = pl.DeviceIdType.MESH
SIDE = 4
ROWS = 256
TOK = 2
LINE_ROWS = 16
PLANE_ROWS = 64
LANES = 128
TURNS = dict(
    x=((0, 2, 1, 3), (0, 3, 2, 1), (0, 3, 1, 2), (0, 1, 2, 3)),
    y=((2, 1, 3, 0), (3, 2, 0, 1), (0, 3, 1, 2), (1, 0, 2, 3)),
    z=((2, 1, 3, 0), (3, 2, 0, 1), (0, 3, 1, 2), (1, 0, 2, 3)),
)
STARTS = dict(x=(0, 2, 1, 3), y=(1, 0, 2, 3), z=(0, 1, 2, 3))
ORDERS = ("xyz", "yzx", "zxy")
UNITS = ((0, 9), (2, 9), (1, 10))
GATED = 0
F32, BF16 = jnp.float32, jnp.bfloat16


def widths():
    offsets, start = [], 0
    for _, blocks in UNITS:
        offsets.append(start)
        start += 2 * blocks * LANES
    return offsets, [blocks * LANES for _, blocks in UNITS]


def row_of(order, at):
    place = dict(x=(at >> 2) & 3, z=(at >> 4) & 3, y=(at >> 6) & 3)
    first, second, third = (place[axis] for axis in ORDERS[order])
    return (((second * SIDE + third) * SIDE + first) << 2) + (at & 3)


def kernel(tok, gates, node_set, wg, wu, wd, out, **r):
    offsets, width = widths()
    n = len(UNITS)

    node, local = lax.axis_index("node"), lax.axis_index("local")
    here = dict(x=local // SIDE, y=local % SIDE, z=node // 2)
    core = node % 2

    def device(axis, step, flip):
        at = dict(here)
        at[axis] = lax.rem(at[axis] + step, SIDE)
        other = lax.rem(core + flip, 2)
        return (at["z"] * 2 + other, at["x"] * SIDE + at["y"])

    depth_at = [sum(width[:u]) for u in range(n)]
    loads = [
        pltpu.make_async_copy(wg, r["wg_v"], r["load_sem"].at[0]),
        pltpu.make_async_copy(wu, r["wu_v"], r["load_sem"].at[1]),
    ]
    for u in range(n):
        mine = pl.ds(pl.multiple_of(offsets[u] + core * width[u], LANES), width[u])
        there = pl.ds(depth_at[u], width[u])
        loads.append(pltpu.make_async_copy(wd.at[:, mine], r["w2"].at[0, :, there], r["load_sem"].at[2]))
    small = [
        pltpu.make_async_copy(gates, r["gates_v"], r["small_sem"].at[0]),
        pltpu.make_async_copy(node_set, r["set_v"], r["small_sem"].at[1]),
    ]
    own = []
    for u in range(n):
        for h in range(2):
            own.append(
                pltpu.make_async_copy(
                    tok.at[:, pl.ds(offsets[u] + h * width[u], width[u])],
                    r["src"][u].at[h, :, pl.ds(0, width[u])],
                    r["tok_sem"].at[u, h],
                )
            )
    for copy in small + own:
        copy.start()

    barrier = pltpu.get_barrier_semaphore()
    partners = [(axis, step, flip) for axis in "xyz" for step in range(1, SIDE) for flip in range(2)]
    partners.append(("x", 0, 1))
    for partner in partners:
        pl.semaphore_signal(barrier, inc=1, device_id=device(*partner), device_id_type=MESH)
    for copy in small:
        copy.wait()
    lane = lax.broadcasted_iota(jnp.int32, (TOK, LANES), 1)
    table = jnp.zeros((TOK, LANES), F32)
    gate_v, set_v = r["gates_v"][...].astype(F32), r["set_v"][...]
    for j in range(set_v.shape[1]):
        pair = jnp.where(lane % 2 == 0, gate_v[:, 2 * j : 2 * j + 1], gate_v[:, 2 * j + 1 : 2 * j + 2])
        table = table + jnp.where(set_v[:, j : j + 1] == lane // 2, pair, 0.0)
    for h in range(2):
        r["src"][GATED][h, :, width[GATED] :] = table.astype(BF16)
    for copy in own:
        copy.wait()
    pl.semaphore_wait(barrier, len(partners))


    def send(src, dst, send_sem, recv_sem, to):
        copy = pltpu.make_async_remote_copy(
            src_ref=src, dst_ref=dst, send_sem=send_sem, recv_sem=recv_sem, device_id=to, device_id_type=MESH
        )
        copy.start()

    def axes(u):
        return ORDERS[UNITS[u][0]]

    def line_slot(u):
        return here[axes(u)[0]] * 2 + core

    for u in range(n):
        for step in (1, 3, 2, 0):
            for flip in range(2):
                if step or flip:
                    send(
                        r["src"][u].at[lax.rem(core + flip, 2)],
                        r["line"][u].at[line_slot(u)],
                        r["p1_send"].at[u],
                        r["p1_recv"].at[u],
                        device(axes(u)[0], step, flip),
                    )
        r["line"][u][pl.ds(line_slot(u), 1)] = r["src"][u][pl.ds(core, 1)]

    def wait_all(ref, sem):
        pltpu.make_async_copy(ref, ref, sem).wait()

    for copy in loads:
        copy.start()
    for u in range(n):
        other = pl.ds(pl.multiple_of(offsets[u] + (1 - core) * width[u], LANES), width[u])
        there = pl.ds(depth_at[u], width[u])
        send(wd.at[:, other], r["w2"].at[1, :, there], r["w_send"], r["w_recv"], device("x", 0, 1))
    down_at = lax.broadcasted_iota(jnp.int32, (ROWS, ROWS), 0)
    across = lax.broadcasted_iota(jnp.int32, (ROWS, ROWS), 1)
    for o in (1, 2):
        r["perm"][o - 1] = (row_of(o, down_at) == across).astype(F32).astype(BF16)
        r["back"][o - 1] = (row_of(o, across) == down_at).astype(F32).astype(BF16)
    def second_block(u, ahead):
        second = lax.rem(here[axes(u)[1]] + ahead, SIDE)
        return pl.ds(pl.multiple_of(second * PLANE_ROWS, PLANE_ROWS), PLANE_ROWS)

    def third_block(u, ahead, step):
        second = lax.rem(here[axes(u)[1]] + ahead, SIDE)
        third = lax.rem(here[axes(u)[2]] + step, SIDE)
        return pl.ds(pl.multiple_of(second * PLANE_ROWS + third * LINE_ROWS, LINE_ROWS), LINE_ROWS)

    def gather3(u, back):
        view = r["rows"][u].at[0, third_block(u, SIDE - back, 0)]
        for step in (2, 1, 3):
            send(view, view, r["p3_send"].at[u], r["p3_recv"].at[u, back], device(axes(u)[2], step, 0))

    for u in range(n):
        wait_all(r["line"][u].at[pl.ds(0, 7)], r["p1_recv"].at[u])
        block = jnp.concatenate([r["line"][u][i].astype(F32) for i in range(8)], axis=0)
        view = r["rows"][u].at[0, third_block(u, 0, 0)]
        view[...] = block.astype(BF16)
        for step in (2, 1, 3):
            send(view, view, r["p2_send"].at[u], r["p2_recv"].at[u, step - 1], device(axes(u)[1], step, 0))
    for u in range(n):
        gather3(u, 0)

    def behind(u, slot):
        axis = axes(u)[1]
        place = None
        for i in range(SIDE):
            there = [p for p in STARTS[axis] if p != i][slot]
            place = there if place is None else jnp.where(here[axis] == i, there, place)
        return lax.rem(here[axis] - place + SIDE, SIDE)

    for slot in range(3):
        for u in range(n):
            back = behind(u, slot)
            wait_all(r["rows"][u].at[0, pl.ds(0, LINE_ROWS)], r["p2_recv"].at[u, back - 1])
            gather3(u, back)
    for slot in range(SIDE):
        for u in range(n):
            back = behind(u, slot - 1) if slot else 0
            wait_all(r["rows"][u].at[0, pl.ds(0, 3 * LINE_ROWS)], r["p3_recv"].at[u, back])
            at = second_block(u, SIDE - back)
            send(
                r["rows"][u].at[0, at],
                r["rows"][u].at[1, at],
                r["s_send"].at[u],
                r["s_recv"].at[u, back],
                device("x", 0, 1),
            )
    for copy in loads[:2]:
        copy.wait()
    for which in range(2):
        for u in range(n):
            if which:
                for step in range(SIDE):
                    wait_all(r["rows"][u].at[1, pl.ds(0, PLANE_ROWS)], r["s_recv"].at[u, step])
            half = core if which == 0 else 1 - core
            depth = pl.ds(pl.multiple_of(offsets[u] + half * width[u], LANES), width[u])
            lhs = r["rows"][u][which, :, : width[u]]
            o = UNITS[u][0]
            for side, weight in enumerate((r["wg_v"], r["wu_v"])):
                part = jnp.dot(lhs, weight[depth, :], preferred_element_type=F32)
                columns = slice(side * 256, side * 256 + 256)
                first = which == 0 and all(UNITS[v][0] != o for v in range(u))
                r["acc"][o, :, columns] = part if first else r["acc"][o, :, columns] + part

    lane = lax.broadcasted_iota(jnp.int32, (ROWS, LANES), 1)
    table = r["rows"][GATED][0, :, width[GATED] :]
    for o in range(3):
        here_table = table if o == 0 else jnp.dot(r["back"][o - 1], table, preferred_element_type=F32)
        for who in range(2):
            expert = (here["z"] * 2 + lax.rem(core + who, 2)) * 2 + local // 8
            column = jnp.sum(jnp.where(lane == expert, here_table.astype(F32), 0.0), axis=1, keepdims=True)
            r["gcol"][who, o] = jnp.broadcast_to(column, (ROWS, LANES))

    total = r["acc"][0]
    for o in (1, 2):
        high = r["acc"][o].astype(BF16)
        low = (r["acc"][o] - high.astype(F32)).astype(BF16)
        total = total + jnp.dot(r["perm"][o - 1], high, preferred_element_type=F32)
        total = total + jnp.dot(r["perm"][o - 1], low, preferred_element_type=F32)
    gate_pre, up_pre = total[:, :256], total[:, 256:]
    hidden = (gate_pre * jax.nn.sigmoid(gate_pre) * up_pre).astype(BF16)
    r["hid"][0, 0] = hidden
    send(r["hid"].at[0, 0], r["hid"].at[1, 0], r["h_send"], r["h_recv"], device("x", 0, 1))

    def down(u, who):
        o = UNITS[u][0]
        weight = r["w2"][who, :, depth_at[u] : depth_at[u] + width[u]]
        part = jnp.dot(r["hid"][who, o], weight, preferred_element_type=F32)
        return part * jnp.concatenate([r["gcol"][who, o]] * UNITS[u][1], axis=1)

    def reorder(who):
        for o in (1, 2):
            r["hid"][who, o] = jnp.dot(r["back"][o - 1], r["hid"][who, 0], preferred_element_type=F32).astype(BF16)

    reorder(0)
    wait_all(r["w2"].at[0], r["load_sem"].at[2])
    wait_all(r["w2"].at[1], r["w_recv"])
    for u in range(n):
        r["own"][u][...] = down(u, 0)
    wait_all(r["hid"].at[1, 0], r["h_recv"])
    reorder(1)
    def turn(u, slot):
        axis = axes(u)[1]
        place = TURNS[axis][0][slot]
        for i in range(1, SIDE):
            place = jnp.where(here[axis] == i, TURNS[axis][i][slot], place)
        return place

    def third_rows(u, place, step):
        third = lax.rem(here[axes(u)[2]] + step, SIDE)
        return pl.ds(pl.multiple_of(place * PLANE_ROWS + third * LINE_ROWS, LINE_ROWS), LINE_ROWS)

    for u in range(n):
        total = r["own"][u][...] + down(u, 1)
        r["own"][u][...] = total
        r["r1_src"][u][...] = total.astype(BF16)
        for slot in range(SIDE):
            for step in (2, 1, 3):
                send(
                    r["r1_src"][u].at[third_rows(u, turn(u, slot), step)],
                    r["r1_dst"][u].at[slot, step - 1],
                    r["r1_send"].at[u],
                    r["r1_recv"].at[u, slot],
                    device(axes(u)[2], step, 0),
                )
    for u in range(n):
        wait_all(r["line"][u].at[pl.ds(0, 7)], r["p1_send"].at[u])
        wait_all(r["rows"][u].at[0, pl.ds(0, 3 * LINE_ROWS)], r["p2_send"].at[u])
        wait_all(r["rows"][u].at[0, pl.ds(0, 3 * PLANE_ROWS)], r["p3_send"].at[u])
        wait_all(r["rows"][u].at[0], r["s_send"].at[u])
    wait_all(r["w2"].at[1], r["w_send"])
    wait_all(r["hid"].at[0, 0], r["h_send"])
    def reduce2(u, slot):
        place = turn(u, slot)
        wait_all(r["r1_dst"][u].at[slot], r["r1_recv"].at[u, slot])
        part = r["own"][u][third_rows(u, place, 0), :]
        for step in range(3):
            part = part + r["r1_dst"][u][slot, step].astype(F32)
        ahead = lax.rem(place + SIDE - here[axes(u)[1]], SIDE)

        @pl.when(ahead == 0)
        def _():
            r["r2_own"][u][...] = part

        @pl.when(ahead != 0)
        def _():
            r["r2_src"][u][slot] = part.astype(BF16)
            send(
                r["r2_src"][u].at[slot],
                r["r2_dst"][u].at[ahead - 1],
                r["r2_send"].at[u],
                r["r2_recv"].at[u],
                device(axes(u)[1], ahead, 0),
            )

    for slot in range(SIDE):
        for u in range(n):
            reduce2(u, slot)
    def reduce3(u):
        wait_all(r["r2_dst"][u], r["r2_recv"].at[u])
        part = r["r2_own"][u][...]
        for step in range(3):
            part = part + r["r2_dst"][u][step].astype(F32)
        for i in range(8):
            r["r3_src"][u][i] = part[2 * i : 2 * i + 2].astype(BF16)
        for step in (2, 1, 3, 0):
            first = lax.rem(here[axes(u)[0]] + step, SIDE)
            for flip in range(2):
                if step or flip:
                    send(
                        r["r3_src"][u].at[first * 2 + lax.rem(core + flip, 2)],
                        r["r3_dst"][u].at[core * SIDE + here[axes(u)[0]]],
                        r["r3_send"].at[u],
                        r["r3_recv"].at[u],
                        device(axes(u)[0], step, flip),
                    )
        r["r3_dst"][u][pl.ds(core * SIDE + here[axes(u)[0]], 1)] = r["r3_src"][u][pl.ds(line_slot(u), 1)]

    for u in range(n):
        pl.when(here[axes(u)[1]] == TURNS[axes(u)[1]][0][0])(functools.partial(reduce3, u))
    for u in range(n):
        pl.when(here[axes(u)[1]] != TURNS[axes(u)[1]][0][0])(functools.partial(reduce3, u))
    for u in range(n):
        wait_all(r["r1_dst"][u], r["r1_send"].at[u])
        wait_all(r["r2_dst"][u], r["r2_send"].at[u])
        wait_all(r["r3_dst"][u].at[pl.ds(0, 7)], r["r3_send"].at[u])
    for u in range(n):
        wait_all(r["r3_dst"][u].at[pl.ds(0, 7)], r["r3_recv"].at[u])
        for h in range(2):
            part = r["r3_dst"][u][h * SIDE].astype(F32)
            for i in range(1, SIDE):
                part = part + r["r3_dst"][u][h * SIDE + i].astype(F32)
            out[:, pl.ds(offsets[u] + h * width[u], width[u])] = part.astype(BF16)


def layer(tokens, gates, node_set, w_gate, w_up, w_down):
    _, width = widths()
    n = len(UNITS)
    whole = [w + (LANES if u == GATED else 0) for u, w in enumerate(width)]
    dma = pltpu.SemaphoreType.DMA
    vmem = pltpu.VMEM
    depth, hidden = w_gate.shape
    scratch = dict(
        gates_v=vmem(gates.shape, BF16),
        set_v=vmem(node_set.shape, jnp.int32),
        wg_v=vmem(w_gate.shape, BF16),
        wu_v=vmem(w_up.shape, BF16),
        w2=vmem((2, hidden, depth // 2), BF16),
        src=[vmem((2, TOK, w), BF16) for w in whole],
        line=[vmem((8, TOK, w), BF16) for w in whole],
        rows=[vmem((2, ROWS, w), BF16) for w in whole],
        acc=vmem((3, ROWS, 2 * hidden), F32),
        hid=vmem((2, 3, ROWS, hidden), BF16),
        gcol=vmem((2, 3, ROWS, LANES), F32),
        perm=vmem((2, ROWS, ROWS), BF16),
        back=vmem((2, ROWS, ROWS), BF16),
        r1_src=[vmem((ROWS, w), BF16) for w in width],
        own=[vmem((ROWS, w), F32) for w in width],
        r1_dst=[vmem((SIDE, 3, LINE_ROWS, w), BF16) for w in width],
        r2_src=[vmem((SIDE, LINE_ROWS, w), BF16) for w in width],
        r2_own=[vmem((LINE_ROWS, w), F32) for w in width],
        r2_dst=[vmem((3, LINE_ROWS, w), BF16) for w in width],
        r3_src=[vmem((8, TOK, w), BF16) for w in width],
        r3_dst=[vmem((8, TOK, w), BF16) for w in width],
        load_sem=dma((3,)),
        tok_sem=dma((n, 2)),
        small_sem=dma((2,)),
        p1_send=dma((n,)),
        p1_recv=dma((n,)),
        p2_send=dma((n,)),
        p2_recv=dma((n, 3)),
        p3_send=dma((n,)),
        p3_recv=dma((n, SIDE)),
        s_send=dma((n,)),
        s_recv=dma((n, SIDE)),
        w_send=dma,
        w_recv=dma,
        h_send=dma,
        h_recv=dma,
        r1_send=dma((n,)),
        r1_recv=dma((n, SIDE)),
        r2_send=dma((n,)),
        r2_recv=dma((n,)),
        r3_send=dma((n,)),
        r3_recv=dma((n,)),
    )
    return pl.pallas_call(
        kernel,
        out_shape=jax.ShapeDtypeStruct(tokens.shape, BF16),
        in_specs=[pl.BlockSpec(memory_space=pl.ANY)] * 6,
        out_specs=pl.BlockSpec(memory_space=pltpu.VMEM),
        scratch_shapes=scratch,
        compiler_params=pltpu.CompilerParams(
            collective_id=0, has_side_effects=True, vmem_limit_bytes=48 << 20
        ),
    )(*[pltpu.with_memory_space_constraint(a, pltpu.HBM) for a in (tokens, gates, node_set, w_gate, w_up, w_down)])


def solution(mesh):
    rows, columns = P(("node", "local"), None), P(None, ("node", "local"))
    return jax.shard_map(
        layer,
        mesh=mesh,
        in_specs=(rows, rows, rows, columns, columns, rows),
        out_specs=rows,
        check_vma=False,
    )
```

```python
import functools

import jax
import jax.numpy as jnp
from jax import lax
from jax.experimental import pallas as pl
from jax.experimental.pallas import tpu as pltpu
from jax.sharding import PartitionSpec as P

MESH = pl.DeviceIdType.MESH
SIDE = 4
ROWS = 256
TOK = 2
LINE_ROWS = 16
PLANE_ROWS = 64
LANES = 128
TURNS = dict(
    x=((0, 2, 1, 3), (0, 3, 2, 1), (0, 3, 1, 2), (0, 1, 2, 3)),
    y=((2, 1, 3, 0), (3, 2, 0, 1), (0, 3, 1, 2), (1, 0, 2, 3)),
    z=((2, 1, 3, 0), (3, 2, 0, 1), (0, 3, 1, 2), (1, 0, 2, 3)),
)
STARTS = dict(x=(0, 2, 1, 3), y=(1, 0, 2, 3), z=(0, 1, 2, 3))
ORDERS = ("xyz", "yzx", "zxy")
UNITS = ((0, 9), (2, 9), (1, 10))
GATED = 0
F32, BF16 = jnp.float32, jnp.bfloat16


def widths():
    offsets, start = [], 0
    for _, blocks in UNITS:
        offsets.append(start)
        start += 2 * blocks * LANES
    return offsets, [blocks * LANES for _, blocks in UNITS]


def row_of(order, at):
    place = dict(x=(at >> 2) & 3, z=(at >> 4) & 3, y=(at >> 6) & 3)
    first, second, third = (place[axis] for axis in ORDERS[order])
    return (((second * SIDE + third) * SIDE + first) << 2) + (at & 3)


def kernel(tok, gates, node_set, wg, wu, wd, out, **r):
    offsets, width = widths()
    n = len(UNITS)

    node, local = lax.axis_index("node"), lax.axis_index("local")
    here = dict(x=local // SIDE, y=local % SIDE, z=node // 2)
    core = node % 2

    def device(axis, step, flip):
        at = dict(here)
        at[axis] = lax.rem(at[axis] + step, SIDE)
        other = lax.rem(core + flip, 2)
        return (at["z"] * 2 + other, at["x"] * SIDE + at["y"])

    depth_at = [sum(width[:u]) for u in range(n)]
    loads = [
        pltpu.make_async_copy(wg, r["wg_v"], r["load_sem"].at[0]),
        pltpu.make_async_copy(wu, r["wu_v"], r["load_sem"].at[1]),
    ]
    for u in range(n):
        mine = pl.ds(pl.multiple_of(offsets[u] + core * width[u], LANES), width[u])
        there = pl.ds(depth_at[u], width[u])
        loads.append(pltpu.make_async_copy(wd.at[:, mine], r["w2"].at[0, :, there], r["load_sem"].at[2]))
    small = [
        pltpu.make_async_copy(gates, r["gates_v"], r["small_sem"].at[0]),
        pltpu.make_async_copy(node_set, r["set_v"], r["small_sem"].at[1]),
    ]
    own = []
    for u in range(n):
        for h in range(2):
            own.append(
                pltpu.make_async_copy(
                    tok.at[:, pl.ds(offsets[u] + h * width[u], width[u])],
                    r["src"][u].at[h, :, pl.ds(0, width[u])],
                    r["tok_sem"].at[u, h],
                )
            )
    for copy in small + own:
        copy.start()

    barrier = pltpu.get_barrier_semaphore()
    partners = [(axis, step, flip) for axis in "xyz" for step in range(1, SIDE) for flip in range(2)]
    partners.append(("x", 0, 1))
    for partner in partners:
        pl.semaphore_signal(barrier, inc=1, device_id=device(*partner), device_id_type=MESH)
    for copy in small:
        copy.wait()
    lane = lax.broadcasted_iota(jnp.int32, (TOK, LANES), 1)
    table = jnp.zeros((TOK, LANES), F32)
    gate_v, set_v = r["gates_v"][...].astype(F32), r["set_v"][...]
    for j in range(set_v.shape[1]):
        pair = jnp.where(lane % 2 == 0, gate_v[:, 2 * j : 2 * j + 1], gate_v[:, 2 * j + 1 : 2 * j + 2])
        table = table + jnp.where(set_v[:, j : j + 1] == lane // 2, pair, 0.0)
    for h in range(2):
        r["src"][GATED][h, :, width[GATED] :] = table.astype(BF16)
    for copy in own:
        copy.wait()
    pl.semaphore_wait(barrier, len(partners))


    def send(src, dst, send_sem, recv_sem, to):
        copy = pltpu.make_async_remote_copy(
            src_ref=src, dst_ref=dst, send_sem=send_sem, recv_sem=recv_sem, device_id=to, device_id_type=MESH
        )
        copy.start()

    def axes(u):
        return ORDERS[UNITS[u][0]]

    def line_slot(u):
        return here[axes(u)[0]] * 2 + core

    for step in (2, 1, 3, 0):
        for u in range(n):
            for flip in range(2):
                if step or flip:
                    send(
                        r["src"][u].at[lax.rem(core + flip, 2)],
                        r["line"][u].at[line_slot(u)],
                        r["p1_send"].at[u],
                        r["p1_recv"].at[u],
                        device(axes(u)[0], step, flip),
                    )
    for u in range(n):
        r["line"][u][pl.ds(line_slot(u), 1)] = r["src"][u][pl.ds(core, 1)]

    def wait_all(ref, sem):
        pltpu.make_async_copy(ref, ref, sem).wait()

    for copy in loads:
        copy.start()
    for u in range(n):
        other = pl.ds(pl.multiple_of(offsets[u] + (1 - core) * width[u], LANES), width[u])
        there = pl.ds(depth_at[u], width[u])
        send(wd.at[:, other], r["w2"].at[1, :, there], r["w_send"], r["w_recv"], device("x", 0, 1))
    down_at = lax.broadcasted_iota(jnp.int32, (ROWS, ROWS), 0)
    across = lax.broadcasted_iota(jnp.int32, (ROWS, ROWS), 1)
    for o in (1, 2):
        r["perm"][o - 1] = (row_of(o, down_at) == across).astype(F32).astype(BF16)
        r["back"][o - 1] = (row_of(o, across) == down_at).astype(F32).astype(BF16)
    def second_block(u, ahead):
        second = lax.rem(here[axes(u)[1]] + ahead, SIDE)
        return pl.ds(pl.multiple_of(second * PLANE_ROWS, PLANE_ROWS), PLANE_ROWS)

    def third_block(u, ahead, step):
        second = lax.rem(here[axes(u)[1]] + ahead, SIDE)
        third = lax.rem(here[axes(u)[2]] + step, SIDE)
        return pl.ds(pl.multiple_of(second * PLANE_ROWS + third * LINE_ROWS, LINE_ROWS), LINE_ROWS)

    def gather3(u, back):
        view = r["rows"][u].at[0, third_block(u, SIDE - back, 0)]
        for step in (2, 1, 3):
            send(view, view, r["p3_send"].at[u], r["p3_recv"].at[u, back], device(axes(u)[2], step, 0))

    for u in range(n):
        wait_all(r["line"][u].at[pl.ds(0, 7)], r["p1_recv"].at[u])
        block = jnp.concatenate([r["line"][u][i].astype(F32) for i in range(8)], axis=0)
        view = r["rows"][u].at[0, third_block(u, 0, 0)]
        view[...] = block.astype(BF16)
        for step in (2, 1, 3):
            send(view, view, r["p2_send"].at[u], r["p2_recv"].at[u, step - 1], device(axes(u)[1], step, 0))
    for u in range(n):
        gather3(u, 0)

    def behind(u, slot):
        axis = axes(u)[1]
        place = None
        for i in range(SIDE):
            there = [p for p in STARTS[axis] if p != i][slot]
            place = there if place is None else jnp.where(here[axis] == i, there, place)
        return lax.rem(here[axis] - place + SIDE, SIDE)

    for slot in range(3):
        for u in range(n):
            back = behind(u, slot)
            wait_all(r["rows"][u].at[0, pl.ds(0, LINE_ROWS)], r["p2_recv"].at[u, back - 1])
            gather3(u, back)
    for slot in range(SIDE):
        for u in range(n):
            back = behind(u, slot - 1) if slot else 0
            wait_all(r["rows"][u].at[0, pl.ds(0, 3 * LINE_ROWS)], r["p3_recv"].at[u, back])
            at = second_block(u, SIDE - back)
            send(
                r["rows"][u].at[0, at],
                r["rows"][u].at[1, at],
                r["s_send"].at[u],
                r["s_recv"].at[u, back],
                device("x", 0, 1),
            )
    for copy in loads[:2]:
        copy.wait()
    for which in range(2):
        for u in range(n):
            if which:
                for step in range(SIDE):
                    wait_all(r["rows"][u].at[1, pl.ds(0, PLANE_ROWS)], r["s_recv"].at[u, step])
            half = core if which == 0 else 1 - core
            depth = pl.ds(pl.multiple_of(offsets[u] + half * width[u], LANES), width[u])
            lhs = r["rows"][u][which, :, : width[u]]
            o = UNITS[u][0]
            for side, weight in enumerate((r["wg_v"], r["wu_v"])):
                part = jnp.dot(lhs, weight[depth, :], preferred_element_type=F32)
                columns = slice(side * 256, side * 256 + 256)
                first = which == 0 and all(UNITS[v][0] != o for v in range(u))
                r["acc"][o, :, columns] = part if first else r["acc"][o, :, columns] + part

    lane = lax.broadcasted_iota(jnp.int32, (ROWS, LANES), 1)
    table = r["rows"][GATED][0, :, width[GATED] :]
    for o in range(3):
        here_table = table if o == 0 else jnp.dot(r["back"][o - 1], table, preferred_element_type=F32)
        for who in range(2):
            expert = (here["z"] * 2 + lax.rem(core + who, 2)) * 2 + local // 8
            column = jnp.sum(jnp.where(lane == expert, here_table.astype(F32), 0.0), axis=1, keepdims=True)
            r["gcol"][who, o] = jnp.broadcast_to(column, (ROWS, LANES))

    total = r["acc"][0]
    for o in (1, 2):
        high = r["acc"][o].astype(BF16)
        low = (r["acc"][o] - high.astype(F32)).astype(BF16)
        total = total + jnp.dot(r["perm"][o - 1], high, preferred_element_type=F32)
        total = total + jnp.dot(r["perm"][o - 1], low, preferred_element_type=F32)
    gate_pre, up_pre = total[:, :256], total[:, 256:]
    hidden = (gate_pre * jax.nn.sigmoid(gate_pre) * up_pre).astype(BF16)
    r["hid"][0, 0] = hidden
    send(r["hid"].at[0, 0], r["hid"].at[1, 0], r["h_send"], r["h_recv"], device("x", 0, 1))

    def down(u, who):
        o = UNITS[u][0]
        weight = r["w2"][who, :, depth_at[u] : depth_at[u] + width[u]]
        part = jnp.dot(r["hid"][who, o], weight, preferred_element_type=F32)
        return part * jnp.concatenate([r["gcol"][who, o]] * UNITS[u][1], axis=1)

    def reorder(who):
        for o in (1, 2):
            r["hid"][who, o] = jnp.dot(r["back"][o - 1], r["hid"][who, 0], preferred_element_type=F32).astype(BF16)

    reorder(0)
    wait_all(r["w2"].at[0], r["load_sem"].at[2])
    wait_all(r["w2"].at[1], r["w_recv"])
    for u in range(n):
        r["own"][u][...] = down(u, 0)
    wait_all(r["hid"].at[1, 0], r["h_recv"])
    reorder(1)
    def turn(u, slot):
        axis = axes(u)[1]
        place = TURNS[axis][0][slot]
        for i in range(1, SIDE):
            place = jnp.where(here[axis] == i, TURNS[axis][i][slot], place)
        return place

    def third_rows(u, place, step):
        third = lax.rem(here[axes(u)[2]] + step, SIDE)
        return pl.ds(pl.multiple_of(place * PLANE_ROWS + third * LINE_ROWS, LINE_ROWS), LINE_ROWS)

    for u in range(n):
        r["r1_src"][u][...] = (r["own"][u][...] + down(u, 1)).astype(BF16)
        for slot in range(SIDE):
            for step in (2, 1, 3):
                send(
                    r["r1_src"][u].at[third_rows(u, turn(u, slot), step)],
                    r["r1_dst"][u].at[slot, step - 1],
                    r["r1_send"].at[u],
                    r["r1_recv"].at[u, slot],
                    device(axes(u)[2], step, 0),
                )
    for u in range(n):
        wait_all(r["line"][u].at[pl.ds(0, 7)], r["p1_send"].at[u])
        wait_all(r["rows"][u].at[0, pl.ds(0, 3 * LINE_ROWS)], r["p2_send"].at[u])
        wait_all(r["rows"][u].at[0, pl.ds(0, 3 * PLANE_ROWS)], r["p3_send"].at[u])
        wait_all(r["rows"][u].at[0], r["s_send"].at[u])
    wait_all(r["w2"].at[1], r["w_send"])
    wait_all(r["hid"].at[0, 0], r["h_send"])
    def reduce2(u, slot):
        place = turn(u, slot)
        wait_all(r["r1_dst"][u].at[slot], r["r1_recv"].at[u, slot])
        part = r["r1_src"][u][third_rows(u, place, 0), :].astype(F32)
        for step in range(3):
            part = part + r["r1_dst"][u][slot, step].astype(F32)
        ahead = lax.rem(place + SIDE - here[axes(u)[1]], SIDE)

        @pl.when(ahead == 0)
        def _():
            r["r2_own"][u][...] = part

        @pl.when(ahead != 0)
        def _():
            r["r2_src"][u][slot] = part.astype(BF16)
            send(
                r["r2_src"][u].at[slot],
                r["r2_dst"][u].at[ahead - 1],
                r["r2_send"].at[u],
                r["r2_recv"].at[u],
                device(axes(u)[1], ahead, 0),
            )

    for slot in range(SIDE):
        for u in range(n):
            reduce2(u, slot)
    def reduce3(u):
        wait_all(r["r2_dst"][u], r["r2_recv"].at[u])
        part = r["r2_own"][u][...]
        for step in range(3):
            part = part + r["r2_dst"][u][step].astype(F32)
        for i in range(8):
            r["r3_src"][u][i] = part[2 * i : 2 * i + 2].astype(BF16)
        for step in (2, 1, 3, 0):
            first = lax.rem(here[axes(u)[0]] + step, SIDE)
            for flip in range(2):
                if step or flip:
                    send(
                        r["r3_src"][u].at[first * 2 + lax.rem(core + flip, 2)],
                        r["r3_dst"][u].at[core * SIDE + here[axes(u)[0]]],
                        r["r3_send"].at[u],
                        r["r3_recv"].at[u],
                        device(axes(u)[0], step, flip),
                    )
        r["r3_dst"][u][pl.ds(core * SIDE + here[axes(u)[0]], 1)] = r["r3_src"][u][pl.ds(line_slot(u), 1)]

    for u in range(n):
        pl.when(here[axes(u)[1]] == TURNS[axes(u)[1]][0][0])(functools.partial(reduce3, u))
    for u in range(n):
        pl.when(here[axes(u)[1]] != TURNS[axes(u)[1]][0][0])(functools.partial(reduce3, u))
    for u in range(n):
        wait_all(r["r1_dst"][u], r["r1_send"].at[u])
        wait_all(r["r2_dst"][u], r["r2_send"].at[u])
        wait_all(r["r3_dst"][u].at[pl.ds(0, 7)], r["r3_send"].at[u])
    for u in range(n):
        wait_all(r["r3_dst"][u].at[pl.ds(0, 7)], r["r3_recv"].at[u])
        for h in range(2):
            part = r["r3_dst"][u][h * SIDE].astype(F32)
            for i in range(1, SIDE):
                part = part + r["r3_dst"][u][h * SIDE + i].astype(F32)
            out[:, pl.ds(offsets[u] + h * width[u], width[u])] = part.astype(BF16)


def layer(tokens, gates, node_set, w_gate, w_up, w_down):
    _, width = widths()
    n = len(UNITS)
    whole = [w + (LANES if u == GATED else 0) for u, w in enumerate(width)]
    dma = pltpu.SemaphoreType.DMA
    vmem = pltpu.VMEM
    depth, hidden = w_gate.shape
    scratch = dict(
        gates_v=vmem(gates.shape, BF16),
        set_v=vmem(node_set.shape, jnp.int32),
        wg_v=vmem(w_gate.shape, BF16),
        wu_v=vmem(w_up.shape, BF16),
        w2=vmem((2, hidden, depth // 2), BF16),
        src=[vmem((2, TOK, w), BF16) for w in whole],
        line=[vmem((8, TOK, w), BF16) for w in whole],
        rows=[vmem((2, ROWS, w), BF16) for w in whole],
        acc=vmem((3, ROWS, 2 * hidden), F32),
        hid=vmem((2, 3, ROWS, hidden), BF16),
        gcol=vmem((2, 3, ROWS, LANES), F32),
        perm=vmem((2, ROWS, ROWS), BF16),
        back=vmem((2, ROWS, ROWS), BF16),
        r1_src=[vmem((ROWS, w), BF16) for w in width],
        own=[vmem((ROWS, w), F32) for w in width],
        r1_dst=[vmem((SIDE, 3, LINE_ROWS, w), BF16) for w in width],
        r2_src=[vmem((SIDE, LINE_ROWS, w), BF16) for w in width],
        r2_own=[vmem((LINE_ROWS, w), F32) for w in width],
        r2_dst=[vmem((3, LINE_ROWS, w), BF16) for w in width],
        r3_src=[vmem((8, TOK, w), BF16) for w in width],
        r3_dst=[vmem((8, TOK, w), BF16) for w in width],
        load_sem=dma((3,)),
        tok_sem=dma((n, 2)),
        small_sem=dma((2,)),
        p1_send=dma((n,)),
        p1_recv=dma((n,)),
        p2_send=dma((n,)),
        p2_recv=dma((n, 3)),
        p3_send=dma((n,)),
        p3_recv=dma((n, SIDE)),
        s_send=dma((n,)),
        s_recv=dma((n, SIDE)),
        w_send=dma,
        w_recv=dma,
        h_send=dma,
        h_recv=dma,
        r1_send=dma((n,)),
        r1_recv=dma((n, SIDE)),
        r2_send=dma((n,)),
        r2_recv=dma((n,)),
        r3_send=dma((n,)),
        r3_recv=dma((n,)),
    )
    return pl.pallas_call(
        kernel,
        out_shape=jax.ShapeDtypeStruct(tokens.shape, BF16),
        in_specs=[pl.BlockSpec(memory_space=pl.ANY)] * 6,
        out_specs=pl.BlockSpec(memory_space=pltpu.VMEM),
        scratch_shapes=scratch,
        compiler_params=pltpu.CompilerParams(
            collective_id=0, has_side_effects=True, vmem_limit_bytes=48 << 20
        ),
    )(*[pltpu.with_memory_space_constraint(a, pltpu.HBM) for a in (tokens, gates, node_set, w_gate, w_up, w_down)])


def solution(mesh):
    rows, columns = P(("node", "local"), None), P(None, ("node", "local"))
    return jax.shard_map(
        layer,
        mesh=mesh,
        in_specs=(rows, rows, rows, columns, columns, rows),
        out_specs=rows,
        check_vma=False,
    )
```

```python
import functools

import jax
import jax.numpy as jnp
from jax import lax
from jax.experimental import pallas as pl
from jax.experimental.pallas import tpu as pltpu
from jax.sharding import PartitionSpec as P

MESH = pl.DeviceIdType.MESH
SIDE = 4
ROWS = 256
TOK = 2
LINE_ROWS = 16
PLANE_ROWS = 64
LANES = 128
TURNS = dict(
    x=((0, 2, 1, 3), (0, 3, 2, 1), (0, 3, 1, 2), (0, 1, 2, 3)),
    y=((2, 1, 3, 0), (3, 2, 0, 1), (0, 3, 1, 2), (1, 0, 2, 3)),
    z=((2, 1, 3, 0), (3, 2, 0, 1), (0, 3, 1, 2), (1, 0, 2, 3)),
)
STARTS = dict(x=(0, 2, 1, 3), y=(1, 0, 2, 3), z=(0, 1, 2, 3))
ORDERS = ("xyz", "yzx", "zxy")
UNITS = ((0, 9), (2, 9), (1, 10))
GATED = 0
F32, BF16 = jnp.float32, jnp.bfloat16


def widths():
    offsets, start = [], 0
    for _, blocks in UNITS:
        offsets.append(start)
        start += 2 * blocks * LANES
    return offsets, [blocks * LANES for _, blocks in UNITS]


def row_of(order, at):
    place = dict(x=(at >> 2) & 3, z=(at >> 4) & 3, y=(at >> 6) & 3)
    first, second, third = (place[axis] for axis in ORDERS[order])
    return (((second * SIDE + third) * SIDE + first) << 2) + (at & 3)


def kernel(tok, gates, node_set, wg, wu, wd, out, **r):
    offsets, width = widths()
    n = len(UNITS)

    node, local = lax.axis_index("node"), lax.axis_index("local")
    here = dict(x=local // SIDE, y=local % SIDE, z=node // 2)
    core = node % 2

    def device(axis, step, flip):
        at = dict(here)
        at[axis] = lax.rem(at[axis] + step, SIDE)
        other = lax.rem(core + flip, 2)
        return (at["z"] * 2 + other, at["x"] * SIDE + at["y"])

    depth_at = [sum(width[:u]) for u in range(n)]
    loads = [
        pltpu.make_async_copy(wg, r["wg_v"], r["load_sem"].at[0]),
        pltpu.make_async_copy(wu, r["wu_v"], r["load_sem"].at[1]),
    ]
    for u in range(n):
        mine = pl.ds(pl.multiple_of(offsets[u] + core * width[u], LANES), width[u])
        there = pl.ds(depth_at[u], width[u])
        loads.append(pltpu.make_async_copy(wd.at[:, mine], r["w2"].at[0, :, there], r["load_sem"].at[2]))
    small = [
        pltpu.make_async_copy(gates, r["gates_v"], r["small_sem"].at[0]),
        pltpu.make_async_copy(node_set, r["set_v"], r["small_sem"].at[1]),
    ]
    own = []
    for u in range(n):
        for h in range(2):
            own.append(
                pltpu.make_async_copy(
                    tok.at[:, pl.ds(offsets[u] + h * width[u], width[u])],
                    r["src"][u].at[h, :, pl.ds(0, width[u])],
                    r["tok_sem"].at[u, h],
                )
            )
    for copy in small + own:
        copy.start()

    barrier = pltpu.get_barrier_semaphore()
    partners = [(axis, step, flip) for step in (2, 1, 3) for axis in "xyz" for flip in range(2)]
    partners.append(("x", 0, 1))
    for partner in partners:
        pl.semaphore_signal(barrier, inc=1, device_id=device(*partner), device_id_type=MESH)
    for copy in small:
        copy.wait()
    lane = lax.broadcasted_iota(jnp.int32, (TOK, LANES), 1)
    table = jnp.zeros((TOK, LANES), F32)
    gate_v, set_v = r["gates_v"][...].astype(F32), r["set_v"][...]
    for j in range(set_v.shape[1]):
        pair = jnp.where(lane % 2 == 0, gate_v[:, 2 * j : 2 * j + 1], gate_v[:, 2 * j + 1 : 2 * j + 2])
        table = table + jnp.where(set_v[:, j : j + 1] == lane // 2, pair, 0.0)
    for h in range(2):
        r["src"][GATED][h, :, width[GATED] :] = table.astype(BF16)
    for copy in own:
        copy.wait()
    pl.semaphore_wait(barrier, len(partners))


    def send(src, dst, send_sem, recv_sem, to):
        copy = pltpu.make_async_remote_copy(
            src_ref=src, dst_ref=dst, send_sem=send_sem, recv_sem=recv_sem, device_id=to, device_id_type=MESH
        )
        copy.start()

    def axes(u):
        return ORDERS[UNITS[u][0]]

    def line_slot(u):
        return here[axes(u)[0]] * 2 + core

    for step in (2, 1, 3, 0):
        for u in range(n):
            for flip in range(2):
                if step or flip:
                    send(
                        r["src"][u].at[lax.rem(core + flip, 2)],
                        r["line"][u].at[line_slot(u)],
                        r["p1_send"].at[u],
                        r["p1_recv"].at[u],
                        device(axes(u)[0], step, flip),
                    )
    for u in range(n):
        r["line"][u][pl.ds(line_slot(u), 1)] = r["src"][u][pl.ds(core, 1)]

    def wait_all(ref, sem):
        pltpu.make_async_copy(ref, ref, sem).wait()

    for copy in loads:
        copy.start()
    for u in range(n):
        other = pl.ds(pl.multiple_of(offsets[u] + (1 - core) * width[u], LANES), width[u])
        there = pl.ds(depth_at[u], width[u])
        send(wd.at[:, other], r["w2"].at[1, :, there], r["w_send"], r["w_recv"], device("x", 0, 1))
    down_at = lax.broadcasted_iota(jnp.int32, (ROWS, ROWS), 0)
    across = lax.broadcasted_iota(jnp.int32, (ROWS, ROWS), 1)
    for o in (1, 2):
        r["perm"][o - 1] = (row_of(o, down_at) == across).astype(F32).astype(BF16)
        r["back"][o - 1] = (row_of(o, across) == down_at).astype(F32).astype(BF16)
    def second_block(u, ahead):
        second = lax.rem(here[axes(u)[1]] + ahead, SIDE)
        return pl.ds(pl.multiple_of(second * PLANE_ROWS, PLANE_ROWS), PLANE_ROWS)

    def third_block(u, ahead, step):
        second = lax.rem(here[axes(u)[1]] + ahead, SIDE)
        third = lax.rem(here[axes(u)[2]] + step, SIDE)
        return pl.ds(pl.multiple_of(second * PLANE_ROWS + third * LINE_ROWS, LINE_ROWS), LINE_ROWS)

    def gather3(u, back):
        view = r["rows"][u].at[0, third_block(u, SIDE - back, 0)]
        for step in (2, 1, 3):
            send(view, view, r["p3_send"].at[u], r["p3_recv"].at[u, back], device(axes(u)[2], step, 0))

    for u in range(n):
        wait_all(r["line"][u].at[pl.ds(0, 7)], r["p1_recv"].at[u])
        block = jnp.concatenate([r["line"][u][i].astype(F32) for i in range(8)], axis=0)
        view = r["rows"][u].at[0, third_block(u, 0, 0)]
        view[...] = block.astype(BF16)
        for step in (2, 1, 3):
            send(view, view, r["p2_send"].at[u], r["p2_recv"].at[u, step - 1], device(axes(u)[1], step, 0))
    for u in range(n):
        gather3(u, 0)

    def behind(u, slot):
        axis = axes(u)[1]
        place = None
        for i in range(SIDE):
            there = [p for p in STARTS[axis] if p != i][slot]
            place = there if place is None else jnp.where(here[axis] == i, there, place)
        return lax.rem(here[axis] - place + SIDE, SIDE)

    for slot in range(3):
        for u in range(n):
            back = behind(u, slot)
            wait_all(r["rows"][u].at[0, pl.ds(0, LINE_ROWS)], r["p2_recv"].at[u, back - 1])
            gather3(u, back)
    for slot in range(SIDE):
        for u in range(n):
            back = behind(u, slot - 1) if slot else 0
            wait_all(r["rows"][u].at[0, pl.ds(0, 3 * LINE_ROWS)], r["p3_recv"].at[u, back])
            at = second_block(u, SIDE - back)
            send(
                r["rows"][u].at[0, at],
                r["rows"][u].at[1, at],
                r["s_send"].at[u],
                r["s_recv"].at[u, back],
                device("x", 0, 1),
            )
    for copy in loads[:2]:
        copy.wait()
    for which in range(2):
        for u in range(n):
            if which:
                for step in range(SIDE):
                    wait_all(r["rows"][u].at[1, pl.ds(0, PLANE_ROWS)], r["s_recv"].at[u, step])
            half = core if which == 0 else 1 - core
            depth = pl.ds(pl.multiple_of(offsets[u] + half * width[u], LANES), width[u])
            lhs = r["rows"][u][which, :, : width[u]]
            o = UNITS[u][0]
            for side, weight in enumerate((r["wg_v"], r["wu_v"])):
                part = jnp.dot(lhs, weight[depth, :], preferred_element_type=F32)
                columns = slice(side * 256, side * 256 + 256)
                first = which == 0 and all(UNITS[v][0] != o for v in range(u))
                r["acc"][o, :, columns] = part if first else r["acc"][o, :, columns] + part

    lane = lax.broadcasted_iota(jnp.int32, (ROWS, LANES), 1)
    table = r["rows"][GATED][0, :, width[GATED] :]
    for o in range(3):
        here_table = table if o == 0 else jnp.dot(r["back"][o - 1], table, preferred_element_type=F32)
        for who in range(2):
            expert = (here["z"] * 2 + lax.rem(core + who, 2)) * 2 + local // 8
            column = jnp.sum(jnp.where(lane == expert, here_table.astype(F32), 0.0), axis=1, keepdims=True)
            r["gcol"][who, o] = jnp.broadcast_to(column, (ROWS, LANES))

    total = r["acc"][0]
    for o in (1, 2):
        high = r["acc"][o].astype(BF16)
        low = (r["acc"][o] - high.astype(F32)).astype(BF16)
        total = total + jnp.dot(r["perm"][o - 1], high, preferred_element_type=F32)
        total = total + jnp.dot(r["perm"][o - 1], low, preferred_element_type=F32)
    gate_pre, up_pre = total[:, :256], total[:, 256:]
    hidden = (gate_pre * jax.nn.sigmoid(gate_pre) * up_pre).astype(BF16)
    r["hid"][0, 0] = hidden
    send(r["hid"].at[0, 0], r["hid"].at[1, 0], r["h_send"], r["h_recv"], device("x", 0, 1))

    def down(u, who):
        o = UNITS[u][0]
        weight = r["w2"][who, :, depth_at[u] : depth_at[u] + width[u]]
        part = jnp.dot(r["hid"][who, o], weight, preferred_element_type=F32)
        return part * jnp.concatenate([r["gcol"][who, o]] * UNITS[u][1], axis=1)

    def reorder(who):
        for o in (1, 2):
            r["hid"][who, o] = jnp.dot(r["back"][o - 1], r["hid"][who, 0], preferred_element_type=F32).astype(BF16)

    reorder(0)
    wait_all(r["w2"].at[0], r["load_sem"].at[2])
    wait_all(r["w2"].at[1], r["w_recv"])
    for u in range(n):
        r["own"][u][...] = down(u, 0)
    wait_all(r["hid"].at[1, 0], r["h_recv"])
    reorder(1)
    def turn(u, slot):
        axis = axes(u)[1]
        place = TURNS[axis][0][slot]
        for i in range(1, SIDE):
            place = jnp.where(here[axis] == i, TURNS[axis][i][slot], place)
        return place

    def third_rows(u, place, step):
        third = lax.rem(here[axes(u)[2]] + step, SIDE)
        return pl.ds(pl.multiple_of(place * PLANE_ROWS + third * LINE_ROWS, LINE_ROWS), LINE_ROWS)

    for u in range(n):
        r["r1_src"][u][...] = (r["own"][u][...] + down(u, 1)).astype(BF16)
        for slot in range(SIDE):
            for step in (2, 1, 3):
                send(
                    r["r1_src"][u].at[third_rows(u, turn(u, slot), step)],
                    r["r1_dst"][u].at[slot, step - 1],
                    r["r1_send"].at[u],
                    r["r1_recv"].at[u, slot],
                    device(axes(u)[2], step, 0),
                )
    for u in range(n):
        wait_all(r["line"][u].at[pl.ds(0, 7)], r["p1_send"].at[u])
        wait_all(r["rows"][u].at[0, pl.ds(0, 3 * LINE_ROWS)], r["p2_send"].at[u])
        wait_all(r["rows"][u].at[0, pl.ds(0, 3 * PLANE_ROWS)], r["p3_send"].at[u])
        wait_all(r["rows"][u].at[0], r["s_send"].at[u])
    wait_all(r["w2"].at[1], r["w_send"])
    wait_all(r["hid"].at[0, 0], r["h_send"])
    def reduce2(u, slot):
        place = turn(u, slot)
        wait_all(r["r1_dst"][u].at[slot], r["r1_recv"].at[u, slot])
        part = r["r1_src"][u][third_rows(u, place, 0), :].astype(F32)
        for step in range(3):
            part = part + r["r1_dst"][u][slot, step].astype(F32)
        ahead = lax.rem(place + SIDE - here[axes(u)[1]], SIDE)

        @pl.when(ahead == 0)
        def _():
            r["r2_own"][u][...] = part

        @pl.when(ahead != 0)
        def _():
            r["r2_src"][u][slot] = part.astype(BF16)
            send(
                r["r2_src"][u].at[slot],
                r["r2_dst"][u].at[ahead - 1],
                r["r2_send"].at[u],
                r["r2_recv"].at[u],
                device(axes(u)[1], ahead, 0),
            )

    for slot in range(SIDE):
        for u in range(n):
            reduce2(u, slot)
    def reduce3(u):
        wait_all(r["r2_dst"][u], r["r2_recv"].at[u])
        part = r["r2_own"][u][...]
        for step in range(3):
            part = part + r["r2_dst"][u][step].astype(F32)
        for i in range(8):
            r["r3_src"][u][i] = part[2 * i : 2 * i + 2].astype(BF16)
        for step in (2, 1, 3, 0):
            first = lax.rem(here[axes(u)[0]] + step, SIDE)
            for flip in range(2):
                if step or flip:
                    send(
                        r["r3_src"][u].at[first * 2 + lax.rem(core + flip, 2)],
                        r["r3_dst"][u].at[core * SIDE + here[axes(u)[0]]],
                        r["r3_send"].at[u],
                        r["r3_recv"].at[u],
                        device(axes(u)[0], step, flip),
                    )
        r["r3_dst"][u][pl.ds(core * SIDE + here[axes(u)[0]], 1)] = r["r3_src"][u][pl.ds(line_slot(u), 1)]

    for u in range(n):
        pl.when(here[axes(u)[1]] == TURNS[axes(u)[1]][0][0])(functools.partial(reduce3, u))
    for u in range(n):
        pl.when(here[axes(u)[1]] != TURNS[axes(u)[1]][0][0])(functools.partial(reduce3, u))
    for u in range(n):
        wait_all(r["r1_dst"][u], r["r1_send"].at[u])
        wait_all(r["r2_dst"][u], r["r2_send"].at[u])
        wait_all(r["r3_dst"][u].at[pl.ds(0, 7)], r["r3_send"].at[u])
    for u in range(n):
        wait_all(r["r3_dst"][u].at[pl.ds(0, 7)], r["r3_recv"].at[u])
        for h in range(2):
            part = r["r3_dst"][u][h * SIDE].astype(F32)
            for i in range(1, SIDE):
                part = part + r["r3_dst"][u][h * SIDE + i].astype(F32)
            out[:, pl.ds(offsets[u] + h * width[u], width[u])] = part.astype(BF16)


def layer(tokens, gates, node_set, w_gate, w_up, w_down):
    _, width = widths()
    n = len(UNITS)
    whole = [w + (LANES if u == GATED else 0) for u, w in enumerate(width)]
    dma = pltpu.SemaphoreType.DMA
    vmem = pltpu.VMEM
    depth, hidden = w_gate.shape
    scratch = dict(
        gates_v=vmem(gates.shape, BF16),
        set_v=vmem(node_set.shape, jnp.int32),
        wg_v=vmem(w_gate.shape, BF16),
        wu_v=vmem(w_up.shape, BF16),
        w2=vmem((2, hidden, depth // 2), BF16),
        src=[vmem((2, TOK, w), BF16) for w in whole],
        line=[vmem((8, TOK, w), BF16) for w in whole],
        rows=[vmem((2, ROWS, w), BF16) for w in whole],
        acc=vmem((3, ROWS, 2 * hidden), F32),
        hid=vmem((2, 3, ROWS, hidden), BF16),
        gcol=vmem((2, 3, ROWS, LANES), F32),
        perm=vmem((2, ROWS, ROWS), BF16),
        back=vmem((2, ROWS, ROWS), BF16),
        r1_src=[vmem((ROWS, w), BF16) for w in width],
        own=[vmem((ROWS, w), F32) for w in width],
        r1_dst=[vmem((SIDE, 3, LINE_ROWS, w), BF16) for w in width],
        r2_src=[vmem((SIDE, LINE_ROWS, w), BF16) for w in width],
        r2_own=[vmem((LINE_ROWS, w), F32) for w in width],
        r2_dst=[vmem((3, LINE_ROWS, w), BF16) for w in width],
        r3_src=[vmem((8, TOK, w), BF16) for w in width],
        r3_dst=[vmem((8, TOK, w), BF16) for w in width],
        load_sem=dma((3,)),
        tok_sem=dma((n, 2)),
        small_sem=dma((2,)),
        p1_send=dma((n,)),
        p1_recv=dma((n,)),
        p2_send=dma((n,)),
        p2_recv=dma((n, 3)),
        p3_send=dma((n,)),
        p3_recv=dma((n, SIDE)),
        s_send=dma((n,)),
        s_recv=dma((n, SIDE)),
        w_send=dma,
        w_recv=dma,
        h_send=dma,
        h_recv=dma,
        r1_send=dma((n,)),
        r1_recv=dma((n, SIDE)),
        r2_send=dma((n,)),
        r2_recv=dma((n,)),
        r3_send=dma((n,)),
        r3_recv=dma((n,)),
    )
    return pl.pallas_call(
        kernel,
        out_shape=jax.ShapeDtypeStruct(tokens.shape, BF16),
        in_specs=[pl.BlockSpec(memory_space=pl.ANY)] * 6,
        out_specs=pl.BlockSpec(memory_space=pltpu.VMEM),
        scratch_shapes=scratch,
        compiler_params=pltpu.CompilerParams(
            collective_id=0, has_side_effects=True, vmem_limit_bytes=48 << 20
        ),
    )(*[pltpu.with_memory_space_constraint(a, pltpu.HBM) for a in (tokens, gates, node_set, w_gate, w_up, w_down)])


def solution(mesh):
    rows, columns = P(("node", "local"), None), P(None, ("node", "local"))
    return jax.shard_map(
        layer,
        mesh=mesh,
        in_specs=(rows, rows, rows, columns, columns, rows),
        out_specs=rows,
        check_vma=False,
    )
```
